128 devices in a mesh: pipe: 4 (over z_lo, core), expert: 32 (over z_hi, x, y).
Axes of the slice: x: 4, y: 4, z: 4 (z_hi: 2, z_lo: 2; z = z_hi * 2 + z_lo), core: 2. Of those that a mesh axis runs over, the one named last changes fastest.
Arguments:
- act_fwd: bfloat16 [4, 2048, 3584], P('pipe', 'expert'), may hold values from -40 to 40
- routes_fwd: int32 [4, 2048, 8], P('pipe', 'expert'), may hold values from 0 to 31, all different within a row; in each aligned block of 64 rows (0 to 63, 64 to 127, ..., all dimensions but the last counted through in order) at most 24 rows name the same one
- mix_fwd: float32 [4, 2048, 8], P('pipe', 'expert'), may hold values from 0.2 to 0.8
- cot_bwd: bfloat16 [4, 2048, 3584], P('pipe', 'expert'), may hold values from -6 to 6
- saved_bwd: bfloat16 [4, 2048, 3584], P('pipe', 'expert'), may hold values from -40 to 40
- routes_bwd: int32 [4, 2048, 8], P('pipe', 'expert'), may hold values from 0 to 31, all different within a row; in each aligned block of 64 rows (0 to 63, 64 to 127, ..., all dimensions but the last counted through in order) at most 24 rows name the same one
- mix_bwd: float32 [4, 2048, 8], P('pipe', 'expert'), may hold values from 0.2 to 0.8
- norm_gain: float32 [4, 3584], P('pipe'), may hold values from 0.5 to 1.5
- w_up: bfloat16 [4, 32, 3584, 1024], P('pipe', 'expert'), may hold values from -0.09375 to 0.09375
- w_down: bfloat16 [4, 32, 1024, 3584], P('pipe', 'expert'), may hold values from -0.1875 to 0.1875
Outputs:
- next_fwd: bfloat16 [4, 2048, 3584], P('pipe', 'expert')
- next_bwd: bfloat16 [4, 2048, 3584], P('pipe', 'expert')
The draws below stay inside these ranges and needn't reach their ends.
Inputs may be any that keep to these rules, and one draw needn't show every extreme that they name: `routes_fwd`: within each section, in each block of 64 consecutive tokens (the tokens of one device) no expert is named by more than 24 tokens, a bound that some block reaches; a token names 8 different experts. `routes_bwd`: as for routes_fwd.
All inputs are finite; a program needn't handle non-finite values.
Results may differ from the reference program's by a relative error of at most 0.006.
Values may be sent and summed in bfloat16 or wider, within the bound.
A program may use at most 128 MiB of HBM per device.

```python
import math
import jax
import jax.numpy as jnp
import numpy as np
from jax import lax

D = 3584
HID = 1024
TOP = 8
ROWS = 64
EXPERTS = 32
TOKENS = 2048
CAP = 24
N_PIPE = 4
N_EXPERT = 32


def rough_field(key, row_lo, row_hi):
    key_body, key_rows, key_cols = jax.random.split(key, 3)
    shape = (N_PIPE, TOKENS, D)
    values = jnp.clip(jax.random.normal(key_body, shape, jnp.float32), -5.0, 5.0)
    row_scale = jnp.exp(jax.random.uniform(key_rows, (N_PIPE, TOKENS, 1), jnp.float32, jnp.log(row_lo), jnp.log(row_hi)))
    col_scale = jnp.exp(jax.random.uniform(key_cols, (D,), jnp.float32, -0.7, 0.7))
    return values * row_scale * col_scale


def draw_act_fwd(key, part):
    key = jax.random.fold_in(key, 11)
    return rough_field(key, 0.3, 3.0).astype(jnp.bfloat16)


def draw_saved_bwd(key, part):
    key = jax.random.fold_in(key, 23)
    return rough_field(key, 0.3, 3.0).astype(jnp.bfloat16)


def level_of(stream_key, dims, cuts, least, high):
    def one(position, parts):
        steps = jax.random.uniform(jax.random.fold_in(jax.random.fold_in(stream_key, 6), position), (parts,), jnp.float32, least / len(cuts), high / len(cuts))
        return jnp.repeat(jnp.exp(steps), dims[position] // parts).reshape((-1,) + (1,) * (len(dims) - position - 1))

    level = one(*cuts[0])
    for cut in cuts[1:]:
        level = level * one(*cut)
    return level


def shared_out(own_key, own, number, rows, number_of, top, reach, skew):
    order = jax.random.permutation(own_key, number_of)
    heavy_load, usual = shares(number_of, rows * top, reach, skew, True), shares(number_of, rows * top, reach, skew, False)
    places = jnp.arange(number_of)

    def named(tallies, turn):
        used = int((tallies > 0).sum())
        fixed = max(1, used // 4)
        passed = fixed + (places - fixed + turn * (used - fixed)) % max(1, number_of - fixed)
        return jnp.zeros((number_of,), jnp.int32).at[order[jnp.where(places < fixed, places, passed)]].set(jnp.asarray(tallies, jnp.int32))

    tallies = jnp.where(number % 4 == 0, named(heavy_load, number // 4), named(usual, number - number // 4 - 1))
    mixed = jax.random.permutation(jax.random.fold_in(own, 3), number_of)
    donor, taker = mixed[0:number_of // 2 * 2:2], mixed[1:number_of // 2 * 2:2]
    slack = jnp.minimum(tallies[donor] - 1, reach - tallies[taker]) // 2
    slack = jnp.where((donor == order[0]) | (taker == order[0]) | (tallies[taker] == 0), 0, jnp.maximum(slack, 0))
    passed = jax.random.randint(jax.random.fold_in(own, 4), (number_of // 2,), 0, 1 << 20) % (slack + 1)
    tallies = tallies.at[donor].add(-passed).at[taker].add(passed)
    labels = jnp.searchsorted(jnp.cumsum(tallies), jnp.arange(rows * top), side="right").astype(jnp.int32)
    table = labels.reshape(top, rows).T
    table = table[jax.random.permutation(jax.random.fold_in(own, 1), rows)]
    turn = jax.random.randint(jax.random.fold_in(own, 2), (rows, 1), 0, top)
    return jnp.take_along_axis(table, (jnp.arange(top)[None, :] + turn) % top, axis=1)


def shares(number_of, total, bound, slope, full):
    portions = [(1 << 20) // math.isqrt(rank ** slope) + 1 for rank in range(1, number_of + 1)]
    largest = bound if full else min(bound, max(-(-total // number_of), total * portions[0] // sum(portions)))
    least = 1 if total - largest >= number_of - 1 else 0
    counts, rest = [largest] + [least] * (number_of - 1), total - largest - least * (number_of - 1)
    while rest > 0:
        candidates = [i for i in range(1, number_of) if counts[i] < largest] or [i for i in range(1, number_of) if counts[i] < bound]
        pool, remaining = sum([portions[i] for i in candidates]), rest
        for i in candidates:
            more = min(bound - counts[i], max(1, remaining * portions[i] // pool), rest)
            counts[i] = counts[i] + more
            rest = rest - more
    return np.array(counts)


def bell_draw(key, shape, spread, limit, pieces=(), held_as=jnp.bfloat16):
    values = spread * jax.random.normal(key, shape, jnp.float32)
    if pieces:
        values = values * level_of(key, shape, pieces, -0.22, 0.18)
    return jnp.clip(values, -limit, limit).astype(held_as)


def setup_inputs(seed: int = 0) -> dict:
    seeds = jax.random.split(jax.random.key(seed), 11)
    act_fwd = draw_act_fwd(jax.random.fold_in(seeds[10], 71), 0)
    routes_fwd_keys = jax.random.split(jax.random.fold_in(seeds[1], 1), N_PIPE * TOKENS // ROWS)
    routes_fwd_turns = jax.random.permutation(jax.random.fold_in(seeds[1], 3), N_PIPE * TOKENS // ROWS)
    routes_fwd = jax.vmap(lambda own, number: shared_out(jax.random.fold_in(seeds[1], 2), own, number, ROWS, EXPERTS, TOP, CAP, 1))(routes_fwd_keys, routes_fwd_turns).reshape((N_PIPE, TOKENS, TOP))
    mix_fwd = jnp.clip(0.2 + 0.6 * jax.random.uniform(seeds[2], (N_PIPE, TOKENS, TOP), jnp.float32) ** level_of(seeds[2], (N_PIPE, TOKENS, TOP), ((0, 4), (1, 32)), -0.2, 0.2), 0.2, 0.8)
    cot_bwd = bell_draw(seeds[3], (N_PIPE, TOKENS, D), 1.0, 6.0, ((0, 4), (1, 32)))
    saved_bwd = draw_saved_bwd(jax.random.fold_in(seeds[10], 71), 0)
    routes_bwd_keys = jax.random.split(jax.random.fold_in(seeds[5], 1), N_PIPE * TOKENS // ROWS)
    routes_bwd_turns = jax.random.permutation(jax.random.fold_in(seeds[5], 3), N_PIPE * TOKENS // ROWS)
    routes_bwd = jax.vmap(lambda own, number: shared_out(jax.random.fold_in(seeds[5], 2), own, number, ROWS, EXPERTS, TOP, CAP, 2))(routes_bwd_keys, routes_bwd_turns).reshape((N_PIPE, TOKENS, TOP))
    mix_bwd = jnp.clip(0.2 + 0.6 * jax.random.uniform(seeds[6], (N_PIPE, TOKENS, TOP), jnp.float32) ** level_of(seeds[6], (N_PIPE, TOKENS, TOP), ((0, 4), (1, 32)), -0.2, 0.2), 0.2, 0.8)
    norm_gain = jnp.clip(1.0 + 0.1 * jax.random.normal(seeds[7], (N_PIPE, D), jnp.float32), 0.5, 1.5)
    w_up = bell_draw(seeds[8], (N_PIPE, EXPERTS, D, HID), D ** -0.5, 0.09375, ((0, 4), (1, 32)))
    w_down = bell_draw(seeds[9], (N_PIPE, EXPERTS, HID, D), HID ** -0.5, 0.1875, ((0, 4), (1, 32)))
    return {"act_fwd": act_fwd, "routes_fwd": routes_fwd, "mix_fwd": mix_fwd, "cot_bwd": cot_bwd, "saved_bwd": saved_bwd, "routes_bwd": routes_bwd, "mix_bwd": mix_bwd, "norm_gain": norm_gain, "w_up": w_up, "w_down": w_down}


def normed(values, gain):
    wide = values.astype(jnp.float32)
    recip = lax.rsqrt(lax.optimization_barrier(jnp.mean(wide * wide, axis=-1, keepdims=True)) + 1e-06)
    scaled = wide * recip
    return (scaled, recip, (scaled * gain).astype(jnp.bfloat16))

def positions(routes, room):
    targets = routes.reshape(-1).astype(jnp.int32)
    one_hot = (targets[:, None] == jnp.arange(EXPERTS, dtype=jnp.int32)[None, :]).astype(jnp.int32)
    before = jnp.cumsum(one_hot, axis=0) - one_hot
    return targets * room + lax.optimization_barrier(jnp.sum(before * one_hot, axis=1))

def forward_expert(items):
    token_rows, up_w, down_w = items
    pre_act = jnp.dot(token_rows, up_w, preferred_element_type=jnp.float32)
    hidden = jax.nn.silu(pre_act).astype(jnp.bfloat16)
    return jnp.dot(hidden, down_w, preferred_element_type=jnp.float32).astype(jnp.bfloat16)

def backward_expert(items):
    token_rows, grad_rows, up_w, down_w = items
    pre_act = jnp.dot(token_rows, up_w, preferred_element_type=jnp.float32)
    sigma = jax.nn.sigmoid(pre_act)
    grad_hidden = jnp.dot(grad_rows, down_w.T, preferred_element_type=jnp.float32)
    grad_pre = (grad_hidden * sigma * (1.0 + pre_act * (1.0 - sigma))).astype(jnp.bfloat16)
    return jnp.dot(grad_pre, up_w.T, preferred_element_type=jnp.float32).astype(jnp.bfloat16)

def one_section(items):
    act, routes_f, mix_f, cot, saved, routes_b, mix_b, gain, up_all, down_all = items
    room = N_EXPERT * CAP
    scaled_f, recip_f, normed_f = normed(act, gain)
    slot_f = positions(routes_f, room)
    buffer_f = jnp.zeros((EXPERTS * room, D), jnp.bfloat16).at[slot_f].set(jnp.repeat(normed_f, TOP, axis=0))
    result_f = lax.map(forward_expert, (buffer_f.reshape(EXPERTS, room, D), up_all, down_all))
    picked_f = result_f.reshape(EXPERTS * room, D)[slot_f].reshape(TOKENS, TOP, D).astype(jnp.float32)
    output = (act.astype(jnp.float32) + lax.optimization_barrier(jnp.sum(mix_f[:, :, None] * picked_f, axis=1))).astype(jnp.bfloat16)
    scaled_b, recip_b, normed_b = normed(saved, gain)
    slot_b = positions(routes_b, room)
    weighted = (mix_b[:, :, None] * cot.astype(jnp.float32)[:, None, :]).astype(jnp.bfloat16).reshape(TOKENS * TOP, D)
    buffer_u = jnp.zeros((EXPERTS * room, D), jnp.bfloat16).at[slot_b].set(jnp.repeat(normed_b, TOP, axis=0))
    buffer_g = jnp.zeros((EXPERTS * room, D), jnp.bfloat16).at[slot_b].set(weighted)
    result_b = lax.map(backward_expert, (buffer_u.reshape(EXPERTS, room, D), buffer_g.reshape(EXPERTS, room, D), up_all, down_all))
    picked_b = result_b.reshape(EXPERTS * room, D)[slot_b].reshape(TOKENS, TOP, D).astype(jnp.float32)
    grad_norm = lax.optimization_barrier(jnp.sum(picked_b, axis=1)) * gain
    grad_x = recip_b * (grad_norm - scaled_b * lax.optimization_barrier(jnp.mean(grad_norm * scaled_b, axis=-1, keepdims=True)))
    grad = (cot.astype(jnp.float32) + grad_x).astype(jnp.bfloat16)
    return (output, grad)

def reference(act_fwd, routes_fwd, mix_fwd, cot_bwd, saved_bwd, routes_bwd, mix_bwd, norm_gain, w_up, w_down):
    outputs, grads = lax.map(one_section, (act_fwd, routes_fwd, mix_fwd, cot_bwd, saved_bwd, routes_bwd, mix_bwd, norm_gain, w_up, w_down))
    return (jnp.roll(outputs, 1, axis=0), jnp.roll(grads, -1, axis=0))
```

```python
import functools

import jax
import jax.numpy as jnp
from jax import lax
from jax.experimental import pallas as pl
from jax.experimental.pallas import tpu as pltpu
from jax.sharding import PartitionSpec as P

MESH = pl.DeviceIdType.MESH
BF, F32 = jnp.bfloat16, jnp.float32

D, HID, TOP, ROWS, CAP = 3584, 1024, 8, 64, 24
SIDE, DEEP = 4, 2
HALF = D // 2
CH = 256
NCH = HALF // CH
PAIR = DEEP * CAP
LINE = SIDE * PAIR
PT = DEEP * ROWS
NOUT, NRET = 3 * NCH, 2 * NCH
RING = 3


def kernel(
    act, routes_f, mix_f, cot, saved, routes_b, mix_b, gain, wup, wdn,
    next_f, next_b,
    ag, rc, snd, wbu, wbd, ob, zb, zr, xb, xr, gs, acc, gh, hid, sel, scl, cw, tab, ttab, yb, gb,
    a_s, a_r, b_s, b_r, c_s, c_r, e_s, e_r, f_s, f_r, g_s, g_r, w_sem, t_s, t_r, p_s, p_r,
):
    pp, me = lax.axis_index("pipe"), lax.axis_index("expert")
    z, x, y = me // (SIDE * SIDE), (me // SIDE) % SIDE, me % SIDE
    n_pipe = lax.axis_size("pipe")

    def device(dz, dx, dy):
        return (pp, ((z + dz) % DEEP) * SIDE * SIDE + ((x + dx) % SIDE) * SIDE + (y + dy) % SIDE)

    gather_at, trade_at = (x, y), (y, x)
    gather_peer = lambda v, k: device(0, k, 0) if v == 0 else device(0, 0, k)
    trade_peer = lambda v, k: device(0, 0, k) if v == 0 else device(0, k, 0)
    other = device(1, 0, 0)
    ahead, behind = ((pp + 1) % n_pipe, me), ((pp + n_pipe - 1) % n_pipe, me)
    shifts = range(1, SIDE)

    def send(src, dst, s_sem, r_sem, to):
        pltpu.make_async_remote_copy(
            src_ref=src, dst_ref=dst, send_sem=s_sem, recv_sem=r_sem, device_id=to, device_id_type=MESH
        ).start()

    def wait(ref, sem):
        pltpu.make_async_copy(ref, ref, sem).wait()

    barrier = pltpu.get_barrier_semaphore()
    peers = [other, ahead, behind] + [gather_peer(v, k) for v in range(2) for k in shifts]
    for peer in peers:
        pl.semaphore_signal(barrier, inc=1, device_id=peer, device_id_type=MESH)

    lane = lax.broadcasted_iota(jnp.int32, (ROWS, 128), 1)
    expert_of = lane % 32
    is_b = (lane // 32) % 2 == 1
    chosen = jnp.zeros((ROWS, 128), F32)
    weight = jnp.zeros((ROWS, 128), F32)
    for k in range(TOP):
        named = jnp.where(is_b, routes_b[:, k : k + 1], routes_f[:, k : k + 1])
        hit = named == expert_of
        chosen = jnp.where(hit, 1.0, chosen)
        weight = jnp.where(hit, jnp.where(is_b, mix_b[:, k : k + 1], mix_f[:, k : k + 1]), weight)
    earlier = lax.broadcasted_iota(jnp.int32, (ROWS, ROWS), 0) > lax.broadcasted_iota(jnp.int32, (ROWS, ROWS), 1)
    rank = jnp.dot(jnp.where(earlier, 1.0, 0.0).astype(BF), chosen.astype(BF), preferred_element_type=F32)
    slot = jnp.where(chosen > 0.5, rank + (z * CAP + 1).astype(F32), 0.0)
    tab[0, x, z] = jnp.where(lane < 64, slot, weight)

    def spread(array, wide):
        for v in range(2):
            for j in range(NCH):
                lo = v * HALF + j * CH
                ag[array * NCH + j, v, gather_at[v], z] = wide[:, lo : lo + CH].astype(BF)

    def normed(ref):
        wide = ref[...].astype(F32)
        recip = lax.rsqrt(jnp.sum(wide * wide, axis=-1, keepdims=True) * (1.0 / D) + 1e-06)
        return wide * recip, recip

    spread(0, normed(saved)[0] * gain[...])

    def stage_a(n):
        for v in range(2):
            own = ag.at[n, v, gather_at[v], z]
            for k in shifts:
                send(own, own, a_s.at[n], a_r.at[n], gather_peer(v, k))

    def stage_b(n):
        six = ag.at[n, 0, pl.ds(0, 3)]
        wait(six, a_r.at[n])
        for v in range(2):
            part = ag.at[n, v, :, z]
            send(part, part, b_s.at[n], b_r.at[n], other)
        wait(six, a_s.at[n])

    def stage_c(n, array):
        batch = 1 if array < 2 else 0
        ring = n % RING
        wait(ag.at[n, 0], b_r.at[n])

        @pl.when(n >= RING)
        def _():
            wait(snd.at[ring], c_s.at[n - RING])

        def one(q, carry):
            for v in range(2):
                rows = ag[n, v, q].reshape(PT, CH)
                got = jnp.dot(sel[batch, v, q], rows, preferred_element_type=F32)
                if array == 1:
                    got = got * scl[v, q][:, 0:1]
                got = got.astype(BF).reshape(SIDE, PAIR, CH)
                if v == 0:
                    rc[n, 0, q, y] = got[0]
                else:
                    rc[n, 1, x, q] = got[0]
                for d in shifts:
                    snd[ring, v, d - 1, q] = got[d]
            return carry

        lax.fori_loop(0, SIDE, one, 0)
        for k in shifts:
            send(snd.at[ring, 0, k - 1], rc.at[n, 0, :, y], c_s.at[n], c_r.at[n], trade_peer(0, k))
            send(snd.at[ring, 1, k - 1], rc.at[n, 1, x], c_s.at[n], c_r.at[n], trade_peer(1, k))
        wait(ag.at[n, 0], b_s.at[n])

    def fetch(step, down):
        j, ring = (step - 3) % NCH, step % 2
        for v in range(2):
            cols = pl.ds(pl.multiple_of(v * HALF + j * CH, CH), CH)
            if down:
                pltpu.make_async_copy(wdn.at[:, cols], wbd.at[ring, v], w_sem.at[ring]).start()
            else:
                pltpu.make_async_copy(wup.at[cols, :], wbu.at[ring, v], w_sem.at[ring]).start()

    def fetched(step, down):
        ring = step % 2
        wait((wbd if down else wbu).at[ring], w_sem.at[ring])
        return ring

    def next_weights(step, last, down):
        @pl.when(step < last)
        def _():
            fetch(step + 1, down)

        @pl.when(step == last)
        def _():
            fetch(step + 1, not down)

    NT = (((1,), (1,)), ((), ()))

    def stage_d(n, ring, down, total):
        six = rc.at[n, :, pl.ds(0, 3)]
        wait(six, c_r.at[n])

        def one(q, carry):
            out = total[q]
            for v in range(2):
                rows = rc[n, v, q].reshape(LINE, CH)
                if down:
                    out = out + lax.dot_general(rows, wbd[ring, v], NT, preferred_element_type=F32)
                else:
                    out = out + jnp.dot(rows, wbu[ring, v], preferred_element_type=F32)
            total[q] = out
            return carry

        lax.fori_loop(0, SIDE, one, 0)

    def stage_e(r, wring, down):
        ring = r % RING

        @pl.when(r >= RING)
        def _():
            wait(ob.at[ring, :, pl.ds(0, 3)], e_s.at[r - RING])

        def one(q, carry):
            for v in range(2):
                if down:
                    got = jnp.dot(hid[q], wbd[wring, v], preferred_element_type=F32)
                else:
                    got = lax.dot_general(hid[q], wbu[wring, v], NT, preferred_element_type=F32)
                ob[ring, v, q] = got.astype(BF).reshape(SIDE, PAIR, CH)
            return carry

        lax.fori_loop(0, SIDE, one, 0)
        for k in shifts:
            send(ob.at[ring, 0, :, (y + k) % SIDE], rc.at[r, 0, SIDE - k], e_s.at[r], e_r.at[r], trade_peer(0, k))
            send(ob.at[ring, 1, (x + k) % SIDE], rc.at[r, 1, SIDE - k], e_s.at[r], e_r.at[r], trade_peer(1, k))
        for q in range(SIDE):
            rc[r, 0, 0, q] = ob[ring, 0, q, y]
        rc[r, 1, 0] = ob[ring, 1, x]

    def stage_f(r):
        ring = r % RING
        unit = r // NCH
        wait(rc.at[r, :, pl.ds(1, 3)], e_r.at[r])

        @pl.when(r >= RING)
        def _():
            wait(zb.at[ring, :, 0], f_s.at[r - RING])

        def one(q, carry):
            for v in range(2):
                rows = rc[r, v, :, q].reshape(LINE, CH)
                both = jnp.dot(cw[unit, v, q], rows, preferred_element_type=F32)
                part = (both[:PT] + both[PT:]).astype(BF).reshape(DEEP, ROWS, CH)
                for zz in range(DEEP):
                    zb[ring, v, zz, q] = part[zz]
            return carry

        lax.fori_loop(0, SIDE, one, 0)
        for v in range(2):
            send(zb.at[ring, v, 1 - z], zr.at[r, v], f_s.at[r], f_r.at[r], other)

    def stage_g(r):
        ring = r % RING
        wait(zr.at[r], f_r.at[r])

        @pl.when(r >= RING)
        def _():
            wait(xb.at[ring, :, pl.ds(0, 3)], g_s.at[r - RING])

        for v in range(2):
            xb[ring, v] = (zb[ring, v, z].astype(F32) + zr[r, v].astype(F32)).astype(BF)
            for k in shifts:
                send(xb.at[ring, v, (gather_at[v] + k) % SIDE], xr.at[r, v, k - 1], g_s.at[r], g_r.at[r], gather_peer(v, k))

    def summed(r, v):
        out = xb[r % RING, v, gather_at[v]].astype(F32)
        for k in range(SIDE - 1):
            out = out + xr[r, v, k].astype(F32)
        return out

    def stage_h_b(r):
        wait(xr.at[r], g_r.at[r])
        for v in range(2):
            gs[r, v] = summed(r, v)

    def stage_h_f(r):
        wait(xr.at[r], g_r.at[r])
        j = r - NCH
        for v in range(2):
            cols = pl.ds(pl.multiple_of(v * HALF + j * CH, CH), CH)
            yb[j, v] = (act[:, cols].astype(F32) + summed(r, v)).astype(BF)
            send(yb.at[j, v], next_f.at[:, cols], p_s.at[0], p_r.at[0], ahead)

    def finish_b():
        scaled, recip = normed(saved)
        total = jnp.zeros((ROWS, 1), F32)
        parts = []
        for v in range(2):
            for j in range(NCH):
                lo = v * HALF + j * CH
                g_n = gs[j, v] * gain[:, lo : lo + CH]
                gs[j, v] = g_n
                total = total + jnp.sum(g_n * scaled[:, lo : lo + CH], axis=-1, keepdims=True)
        mean = total * (1.0 / D)
        for v in range(2):
            for j in range(NCH):
                lo = v * HALF + j * CH
                g_x = recip * (gs[j, v] - scaled[:, lo : lo + CH] * mean)
                gb[:, lo : lo + CH] = (cot[:, lo : lo + CH].astype(F32) + g_x).astype(BF)
        send(gb, next_b, p_s.at[1], p_r.at[1], behind)

    pl.semaphore_wait(barrier, len(peers))
    send(tab.at[0, x, z], tab.at[0, x, z], t_s.at[0], t_r.at[0], other)
    stage_a(0)
    fetch(3, False)
    spread(1, cot[...])
    stage_a(1)
    wait(tab.at[0, 0, 0], t_r.at[0])
    wait(tab.at[0, 0, 0], t_s.at[0])
    tab[1, y] = tab[0, x]
    for v in range(2):
        for k in shifts:
            send(tab.at[v, gather_at[v]], tab.at[v, gather_at[v]], t_s.at[1], t_r.at[1], gather_peer(v, k))
    stage_b(0)
    spread(2, normed(act)[0] * gain[...])
    stage_b(1)
    stage_a(2)
    acc[...] = jnp.zeros_like(acc)
    gh[...] = jnp.zeros_like(gh)
    six = tab.at[:, pl.ds(0, 3)]
    wait(six, t_r.at[1])
    wait(six, t_s.at[1])

    slot_row = lax.broadcasted_iota(jnp.int32, (PAIR, 128), 0).astype(F32) + 1.0
    token_lane = lax.broadcasted_iota(jnp.int32, (PT, 128), 1)
    w_lane = lax.broadcasted_iota(jnp.int32, (PT, LINE), 1)
    w_slot = (w_lane % PAIR).astype(F32) + 1.0

    def tables(q, carry):
        for v in range(2):
            pair = tab[v, q].reshape(PT, 128)
            ttab[v] = pair.T
            col = [jnp.zeros((PT, LINE), F32) for _ in range(3)]
            for d in range(SIDE):
                if v == 0:
                    e = z * SIDE * SIDE + x * SIDE + (y + d) % SIDE
                else:
                    e = z * SIDE * SIDE + ((x + d) % SIDE) * SIDE + y
                for batch in range(2):
                    hit = ttab[v, pl.ds(e + 32 * batch, 1), :] == slot_row
                    sel[batch, v, q, d * PAIR : (d + 1) * PAIR, :] = jnp.where(hit, 1.0, 0.0).astype(BF)
                    if batch == 1:
                        gate = jnp.where(hit, ttab[v, pl.ds(e + 96, 1), :], 0.0)
                        scl[v, q, d * PAIR : (d + 1) * PAIR, :] = jnp.broadcast_to(
                            jnp.sum(gate, axis=1, keepdims=True), (PAIR, 128)
                        )
                here = w_lane // PAIR == d
                for i, first in enumerate((0, 32, 64)):
                    one = jnp.sum(jnp.where(token_lane == e + first, pair, 0.0), axis=1, keepdims=True)
                    col[i] = jnp.where(here, one, col[i])
            hit_f = jnp.where(col[0] == w_slot, col[2], 0.0)
            high = hit_f.astype(BF)
            cw[1, v, q, :PT] = high
            cw[1, v, q, PT:] = (hit_f - high.astype(F32)).astype(BF)
            cw[0, v, q, :PT] = jnp.where(col[1] == w_slot, 1.0, 0.0).astype(BF)
            cw[0, v, q, PT:] = jnp.zeros((PT, LINE), BF)
        return carry

    lax.fori_loop(0, SIDE, tables, 0)
    stage_c(0, 0)

    s1 = 3 + NCH
    s2 = s1 + NCH
    s3 = s2 + NCH
    s4 = s3 + NCH

    def loop1(s, carry):
        stage_b(s - 1)
        stage_a(s)

        @pl.when(s - 2 < NCH)
        def _():
            stage_c(s - 2, 0)

        @pl.when(s - 2 >= NCH)
        def _():
            stage_c(s - 2, 1)

        next_weights(s, s1 - 1, False)
        stage_d(s - 3, fetched(s, False), False, acc)
        return carry

    lax.fori_loop(3, s1, loop1, 0)

    def loop2(s, carry):
        stage_b(s - 1)
        stage_a(s)

        @pl.when(s - 2 < 2 * NCH)
        def _():
            stage_c(s - 2, 1)

        @pl.when(s - 2 >= 2 * NCH)
        def _():
            stage_c(s - 2, 2)

        next_weights(s, s2 - 1, True)
        stage_d(s - 3, fetched(s, True), True, gh)
        return carry

    lax.fori_loop(s1, s2, loop2, 0)

    def between_b(q, carry):
        p = acc[q]
        sigma = jax.nn.sigmoid(p)
        hid[q] = (gh[q] * sigma * (1.0 + p * (1.0 - sigma))).astype(BF)
        acc[q] = jnp.zeros_like(p)
        return carry

    lax.fori_loop(0, SIDE, between_b, 0)

    def back(s):
        r = s - s2

        @pl.when(r >= 1)
        def _():
            stage_f(r - 1)

        @pl.when(r >= 2)
        def _():
            stage_g(r - 2)

    def loop3(s, carry):
        @pl.when(s - 1 < NOUT)
        def _():
            stage_b(s - 1)

        @pl.when(s < NOUT)
        def _():
            stage_a(s)

        @pl.when(s - 2 < NOUT)
        def _():
            stage_c(s - 2, 2)

        next_weights(s, s3 - 1, False)
        ring = fetched(s, False)
        stage_e(s - s2, ring, False)
        stage_d(s - 3, ring, False, acc)
        back(s)

        @pl.when(s - s2 >= 3)
        def _():
            stage_h_b(s - s2 - 3)

        return carry

    lax.fori_loop(s2, s3, loop3, 0)

    def between_f(q, carry):
        p = acc[q]
        hid[q] = (p * jax.nn.sigmoid(p)).astype(BF)
        return carry

    lax.fori_loop(0, SIDE, between_f, 0)

    def loop4(s, carry):
        @pl.when(s < s4 - 1)
        def _():
            fetch(s + 1, True)

        ring = fetched(s, True)
        stage_e(s - s2, ring, True)
        back(s)
        r = s - s2 - 3

        @pl.when(r < NCH)
        def _():
            stage_h_b(r)

        @pl.when(r >= NCH)
        def _():
            stage_h_f(r)

        @pl.when(r == NCH)
        def _():
            finish_b()

        return carry

    lax.fori_loop(s3, s4, loop4, 0)
    stage_f(NRET - 1)
    stage_g(NRET - 2)
    stage_h_f(NRET - 3)
    stage_g(NRET - 1)
    stage_h_f(NRET - 2)
    stage_h_f(NRET - 1)

    for n in range(NOUT - RING, NOUT):
        wait(snd.at[n % RING], c_s.at[n])
    for r in range(NRET - RING, NRET):
        wait(ob.at[r % RING, :, pl.ds(0, 3)], e_s.at[r])
        wait(zb.at[r % RING, :, 0], f_s.at[r])
        wait(xb.at[r % RING, :, pl.ds(0, 3)], g_s.at[r])
    wait(gb, p_s.at[0])
    wait(gb, p_s.at[1])
    wait(next_f, p_r.at[0])
    wait(next_b, p_r.at[1])


def per_device(
    act_fwd, routes_fwd, mix_fwd, cot_bwd, saved_bwd, routes_bwd, mix_bwd, norm_gain, w_up, w_down
):
    vmem, far = pl.BlockSpec(memory_space=pltpu.VMEM), pl.BlockSpec(memory_space=pl.ANY)
    sems = [pltpu.SemaphoreType.DMA((NOUT,))] * 6 + [pltpu.SemaphoreType.DMA((NRET,))] * 6
    sems += [pltpu.SemaphoreType.DMA((2,))] * 5
    out = jax.ShapeDtypeStruct((ROWS, D), BF)
    next_fwd, next_bwd = pl.pallas_call(
        kernel,
        out_shape=(out, out),
        in_specs=[vmem] * 8 + [far] * 2,
        out_specs=(far, far),
        scratch_shapes=[
            pltpu.VMEM((NOUT, 2, SIDE, DEEP, ROWS, CH), BF),
            pltpu.VMEM((NOUT, 2, SIDE, SIDE, PAIR, CH), BF),
            pltpu.VMEM((RING, 2, SIDE - 1, SIDE, PAIR, CH), BF),
            pltpu.VMEM((2, 2, CH, HID), BF),
            pltpu.VMEM((2, 2, HID, CH), BF),
            pltpu.VMEM((RING, 2, SIDE, SIDE, PAIR, CH), BF),
            pltpu.VMEM((RING, 2, DEEP, SIDE, ROWS, CH), BF),
            pltpu.VMEM((NRET, 2, SIDE, ROWS, CH), BF),
            pltpu.VMEM((RING, 2, SIDE, ROWS, CH), BF),
            pltpu.VMEM((NRET, 2, SIDE - 1, ROWS, CH), BF),
            pltpu.VMEM((NCH, 2, ROWS, CH), F32),
            pltpu.VMEM((SIDE, LINE, HID), F32),
            pltpu.VMEM((SIDE, LINE, HID), F32),
            pltpu.VMEM((SIDE, LINE, HID), BF),
            pltpu.VMEM((2, 2, SIDE, LINE, PT), BF),
            pltpu.VMEM((2, SIDE, LINE, 128), F32),
            pltpu.VMEM((2, 2, SIDE, 2 * PT, LINE), BF),
            pltpu.VMEM((2, SIDE, DEEP, ROWS, 128), F32),
            pltpu.VMEM((2, 128, 128), F32),
            pltpu.VMEM((NCH, 2, ROWS, CH), BF),
            pltpu.VMEM((ROWS, D), BF),
        ]
        + sems,
        compiler_params=pltpu.CompilerParams(
            collective_id=0, has_side_effects=True, vmem_limit_bytes=63 * 2**20
        ),
        cost_estimate=pl.CostEstimate(flops=30 * 10**9, bytes_accessed=40 * 10**6, transcendentals=2 * 10**6),
    )(
        act_fwd[0], routes_fwd[0], mix_fwd[0], cot_bwd[0], saved_bwd[0], routes_bwd[0], mix_bwd[0],
        norm_gain, w_up[0, 0], w_down[0, 0],
    )
    return next_fwd[None], next_bwd[None]


def solution(mesh):
    rows = P("pipe", "expert", None)
    return jax.shard_map(
        per_device,
        mesh=mesh,
        in_specs=(rows,) * 7 + (P("pipe", None),) + (P("pipe", "expert", None, None),) * 2,
        out_specs=(rows, rows),
        check_vma=False,
    )
```

```python
import functools

import jax
import jax.numpy as jnp
from jax import lax
from jax.experimental import pallas as pl
from jax.experimental.pallas import tpu as pltpu
from jax.sharding import PartitionSpec as P

MESH = pl.DeviceIdType.MESH
BF, F32 = jnp.bfloat16, jnp.float32

D, HID, TOP, ROWS, CAP = 3584, 1024, 8, 64, 24
SIDE, DEEP = 4, 2
HALF = D // 2
CH = 256
NCH = HALF // CH
PAIR = DEEP * CAP
LINE = SIDE * PAIR
PT = DEEP * ROWS
NOUT, NRET = 3 * NCH, 2 * NCH
RING_S, RING_O, RING_Z, RING_X = 3, 4, 4, 8
AT_A, AT_B, AT_C, AT_D = 0, 2, 4, 6
AT_F, AT_G, AT_H = AT_D + 2 * NCH + 3, AT_D + 2 * NCH + 6, AT_D + 2 * NCH + 10


def kernel(
    act, routes_f, mix_f, cot, saved, routes_b, mix_b, gain, wup, wdn,
    next_f, next_b,
    ag, rc, snd, wbu, wbd, ob, zb, zr, xb, xr, gs, acc, gh, hid, sel, scl, cw, tab, ttab, yb, gb,
    a_s, a_r, b_s, b_r, c_s, c_r, e_s, e_r, f_s, f_r, g_s, g_r, w_sem, t_s, t_r, p_s, p_r,
):
    pp, me = lax.axis_index("pipe"), lax.axis_index("expert")
    z, x, y = me // (SIDE * SIDE), (me // SIDE) % SIDE, me % SIDE
    n_pipe = lax.axis_size("pipe")

    def device(dz, dx, dy):
        return (pp, ((z + dz) % DEEP) * SIDE * SIDE + ((x + dx) % SIDE) * SIDE + (y + dy) % SIDE)

    gather_at, trade_at = (x, y), (y, x)
    gather_peer = lambda v, k: device(0, k, 0) if v == 0 else device(0, 0, k)
    trade_peer = lambda v, k: device(0, 0, k) if v == 0 else device(0, k, 0)
    other = device(1, 0, 0)
    ahead, behind = ((pp + 1) % n_pipe, me), ((pp + n_pipe - 1) % n_pipe, me)
    shifts = range(1, SIDE)

    def send(src, dst, s_sem, r_sem, to):
        pltpu.make_async_remote_copy(
            src_ref=src, dst_ref=dst, send_sem=s_sem, recv_sem=r_sem, device_id=to, device_id_type=MESH
        ).start()

    def wait(ref, sem):
        pltpu.make_async_copy(ref, ref, sem).wait()

    barrier = pltpu.get_barrier_semaphore()
    peers = [other, ahead, behind] + [gather_peer(v, k) for v in range(2) for k in shifts]
    for peer in peers:
        pl.semaphore_signal(barrier, inc=1, device_id=peer, device_id_type=MESH)

    line = lax.broadcasted_iota(jnp.int32, (128, ROWS), 0)
    expert_of = line % 32
    is_b = (line // 32) % 2 == 1
    chosen = jnp.zeros((128, ROWS), F32)
    weight = jnp.zeros((128, ROWS), F32)
    for k in range(TOP):
        named = jnp.where(is_b, routes_b[k : k + 1, :], routes_f[k : k + 1, :])
        hit = named == expert_of
        chosen = jnp.where(hit, 1.0, chosen)
        weight = jnp.where(hit, jnp.where(is_b, mix_b[k : k + 1, :], mix_f[k : k + 1, :]), weight)
    earlier = lax.broadcasted_iota(jnp.int32, (ROWS, ROWS), 0) < lax.broadcasted_iota(jnp.int32, (ROWS, ROWS), 1)
    rank = jnp.dot(chosen.astype(BF), jnp.where(earlier, 1.0, 0.0).astype(BF), preferred_element_type=F32)
    slot = jnp.where(chosen > 0.5, rank + (z * CAP + 1).astype(F32), 0.0)
    tab[0, x, z] = jnp.where(line < 64, slot, weight).T

    def spread(array, wide):
        for v in range(2):
            for j in range(NCH):
                lo = v * HALF + j * CH
                ag[array * NCH + j, v, gather_at[v], z] = wide[:, lo : lo + CH].astype(BF)

    def normed(ref):
        wide = ref[...].astype(F32)
        recip = lax.rsqrt(jnp.sum(wide * wide, axis=-1, keepdims=True) * (1.0 / D) + 1e-06)
        return wide * recip, recip

    spread(0, normed(saved)[0] * gain[...])

    def stage_a(n):
        for v in range(2):
            own = ag.at[n, v, gather_at[v], z]
            for k in shifts:
                send(own, own, a_s.at[n], a_r.at[n], gather_peer(v, k))

    def stage_b(n):
        six = ag.at[n, 0, pl.ds(0, 3)]
        wait(six, a_r.at[n])
        for v in range(2):
            part = ag.at[n, v, :, z]
            send(part, part, b_s.at[n], b_r.at[n], other)

    def stage_c(n, array):
        batch = 1 if array < 2 else 0
        ring = n % RING_S
        wait(ag.at[n, 0], b_r.at[n])

        @pl.when(n >= RING_S)
        def _():
            wait(snd.at[ring], c_s.at[n - RING_S])

        def one(q, carry):
            for v in range(2):
                rows = ag[n, v, q].reshape(PT, CH)
                got = jnp.dot(sel[batch, v, q], rows, preferred_element_type=F32)
                if array == 1:
                    got = got * scl[v, q][:, 0:1]
                got = got.astype(BF).reshape(SIDE, PAIR, CH)
                if v == 0:
                    rc[n, 0, q, y] = got[0]
                else:
                    rc[n, 1, x, q] = got[0]
                for d in shifts:
                    snd[ring, v, d - 1, q] = got[d]
            return carry

        lax.fori_loop(0, SIDE, one, 0)
        for k in shifts:
            send(snd.at[ring, 0, k - 1], rc.at[n, 0, :, y], c_s.at[n], c_r.at[n], trade_peer(0, k))
            send(snd.at[ring, 1, k - 1], rc.at[n, 1, x], c_s.at[n], c_r.at[n], trade_peer(1, k))

    def fetch(i, down):
        j, ring = i % NCH, i % 2
        for v in range(2):
            cols = pl.ds(pl.multiple_of(v * HALF + j * CH, CH), CH)
            if down:
                pltpu.make_async_copy(wdn.at[:, cols], wbd.at[ring, v], w_sem.at[ring]).start()
            else:
                pltpu.make_async_copy(wup.at[cols, :], wbu.at[ring, v], w_sem.at[ring]).start()

    NT = (((1,), (1,)), ((), ()))

    def stage_d(n, down, total):
        ring = n % 2
        six = rc.at[n, :, pl.ds(0, 3)]
        wait(six, c_r.at[n])

        def one(q, carry):
            out = total[q]
            for v in range(2):
                rows = rc[n, v, q].reshape(LINE, CH)
                if down:
                    out = out + lax.dot_general(rows, wbd[ring, v], NT, preferred_element_type=F32)
                else:
                    out = out + jnp.dot(rows, wbu[ring, v], preferred_element_type=F32)
            total[q] = out
            return carry

        lax.fori_loop(0, SIDE, one, 0)

    def stage_e(r, down):
        ring, wring = r % RING_O, r % 2

        @pl.when(r >= RING_O)
        def _():
            wait(ob.at[ring, :, pl.ds(0, 3)], e_s.at[r - RING_O])

        def one(q, carry):
            for v in range(2):
                if down:
                    got = jnp.dot(hid[q], wbd[wring, v], preferred_element_type=F32)
                else:
                    got = lax.dot_general(hid[q], wbu[wring, v], NT, preferred_element_type=F32)
                ob[ring, v, q] = got.astype(BF).reshape(SIDE, PAIR, CH)
            return carry

        lax.fori_loop(0, SIDE, one, 0)
        for k in shifts:
            send(ob.at[ring, 0, :, (y + k) % SIDE], rc.at[r, 0, SIDE - k], e_s.at[r], e_r.at[r], trade_peer(0, k))
            send(ob.at[ring, 1, (x + k) % SIDE], rc.at[r, 1, SIDE - k], e_s.at[r], e_r.at[r], trade_peer(1, k))
        for q in range(SIDE):
            rc[r, 0, 0, q] = ob[ring, 0, q, y]
        rc[r, 1, 0] = ob[ring, 1, x]

    def stage_f(r):
        ring = r % RING_Z
        unit = r // NCH
        wait(rc.at[r, :, pl.ds(1, 3)], e_r.at[r])

        @pl.when(r >= RING_Z)
        def _():
            wait(zb.at[ring, :, 0], f_s.at[r - RING_Z])

        def one(q, carry):
            for v in range(2):
                rows = rc[r, v, :, q].reshape(LINE, CH)
                both = jnp.dot(cw[unit, v, q], rows, preferred_element_type=F32)
                part = (both[:PT] + both[PT:]).astype(BF).reshape(DEEP, ROWS, CH)
                for zz in range(DEEP):
                    zb[ring, v, zz, q] = part[zz]
            return carry

        lax.fori_loop(0, SIDE, one, 0)
        for v in range(2):
            send(zb.at[ring, v, 1 - z], zr.at[r, v], f_s.at[r], f_r.at[r], other)

    def stage_g(r):
        ring, zring = r % RING_X, r % RING_Z
        wait(zr.at[r], f_r.at[r])

        @pl.when(r >= RING_X)
        def _():
            wait(xb.at[ring, :, pl.ds(0, 3)], g_s.at[r - RING_X])

        for v in range(2):
            xb[ring, v] = (zb[zring, v, z].astype(F32) + zr[r, v].astype(F32)).astype(BF)
            for k in shifts:
                send(xb.at[ring, v, (gather_at[v] + k) % SIDE], xr.at[r, v, k - 1], g_s.at[r], g_r.at[r], gather_peer(v, k))

    def summed(r, v):
        out = xb[r % RING_X, v, gather_at[v]].astype(F32)
        for k in range(SIDE - 1):
            out = out + xr[r, v, k].astype(F32)
        return out

    def stage_h_b(r):
        wait(xr.at[r], g_r.at[r])
        for v in range(2):
            gs[r, v] = summed(r, v)

    def stage_h_f(r):
        wait(xr.at[r], g_r.at[r])
        j = r - NCH
        for v in range(2):
            cols = pl.ds(pl.multiple_of(v * HALF + j * CH, CH), CH)
            yb[j, v] = (act[:, cols].astype(F32) + summed(r, v)).astype(BF)
            send(yb.at[j, v], next_f.at[:, cols], p_s.at[0], p_r.at[0], ahead)

    def finish_b():
        scaled, recip = normed(saved)
        total = jnp.zeros((ROWS, 1), F32)
        parts = []
        for v in range(2):
            for j in range(NCH):
                lo = v * HALF + j * CH
                g_n = gs[j, v] * gain[:, lo : lo + CH]
                gs[j, v] = g_n
                total = total + jnp.sum(g_n * scaled[:, lo : lo + CH], axis=-1, keepdims=True)
        mean = total * (1.0 / D)
        for v in range(2):
            for j in range(NCH):
                lo = v * HALF + j * CH
                g_x = recip * (gs[j, v] - scaled[:, lo : lo + CH] * mean)
                gb[:, lo : lo + CH] = (cot[:, lo : lo + CH].astype(F32) + g_x).astype(BF)
        send(gb, next_b, p_s.at[1], p_r.at[1], behind)

    def when(condition, stage, *args):
        pl.when(condition)(lambda: stage(*args))

    def within(i, lo, hi):
        return jnp.logical_and(i >= lo, i < hi)

    pl.semaphore_wait(barrier, len(peers))
    send(tab.at[0, x, z], tab.at[0, x, z], t_s.at[0], t_r.at[0], other)
    stage_a(0)
    fetch(0, False)
    spread(1, cot[...])
    wait(tab.at[0, 0, 0], t_r.at[0])
    wait(tab.at[0, 0, 0], t_s.at[0])
    tab[1, y] = tab[0, x]
    for v in range(2):
        for k in shifts:
            send(tab.at[v, gather_at[v]], tab.at[v, gather_at[v]], t_s.at[1], t_r.at[1], gather_peer(v, k))
    spread(2, normed(act)[0] * gain[...])
    acc[...] = jnp.zeros_like(acc)
    gh[...] = jnp.zeros_like(gh)

    slot_row = lax.broadcasted_iota(jnp.int32, (PAIR, 128), 0).astype(F32) + 1.0
    token_lane = lax.broadcasted_iota(jnp.int32, (PT, 128), 1)
    w_lane = lax.broadcasted_iota(jnp.int32, (PT, LINE), 1)
    w_slot = (w_lane % PAIR).astype(F32) + 1.0

    def one_table(q, carry):
        for v in range(2):
            pair = tab[v, q].reshape(PT, 128)
            ttab[v] = pair.T
            col = [jnp.zeros((PT, LINE), F32) for _ in range(3)]
            for d in range(SIDE):
                if v == 0:
                    e = z * SIDE * SIDE + x * SIDE + (y + d) % SIDE
                else:
                    e = z * SIDE * SIDE + ((x + d) % SIDE) * SIDE + y
                for batch in range(2):
                    hit = ttab[v, pl.ds(e + 32 * batch, 1), :] == slot_row
                    sel[batch, v, q, d * PAIR : (d + 1) * PAIR, :] = jnp.where(hit, 1.0, 0.0).astype(BF)
                    if batch == 1:
                        gate = jnp.where(hit, ttab[v, pl.ds(e + 96, 1), :], 0.0)
                        scl[v, q, d * PAIR : (d + 1) * PAIR, :] = jnp.broadcast_to(
                            jnp.sum(gate, axis=1, keepdims=True), (PAIR, 128)
                        )
                here = w_lane // PAIR == d
                for i, first in enumerate((0, 32, 64)):
                    one = jnp.sum(jnp.where(token_lane == e + first, pair, 0.0), axis=1, keepdims=True)
                    col[i] = jnp.where(here, one, col[i])
            hit_f = jnp.where(col[0] == w_slot, col[2], 0.0)
            high = hit_f.astype(BF)
            cw[1, v, q, :PT] = high
            cw[1, v, q, PT:] = (hit_f - high.astype(F32)).astype(BF)
            cw[0, v, q, :PT] = jnp.where(col[1] == w_slot, 1.0, 0.0).astype(BF)
            cw[0, v, q, PT:] = jnp.zeros((PT, LINE), BF)
        return carry

    def tables():
        six = tab.at[:, pl.ds(0, 3)]
        wait(six, t_r.at[1])
        wait(six, t_s.at[1])
        lax.fori_loop(0, SIDE, one_table, 0)

    def between_b():
        def one(q, carry):
            p = acc[q]
            sigma = jax.nn.sigmoid(p)
            hid[q] = (gh[q] * sigma * (1.0 + p * (1.0 - sigma))).astype(BF)
            acc[q] = jnp.zeros_like(p)
            return carry

        lax.fori_loop(0, SIDE, one, 0)

    def between_f():
        def one(q, carry):
            p = acc[q]
            hid[q] = (p * jax.nn.sigmoid(p)).astype(BF)
            return carry

        lax.fori_loop(0, SIDE, one, 0)

    def step(s, carry):
        when(within(s - AT_B, 0, NOUT), stage_b, s - AT_B)
        when(within(s - AT_F, 0, NRET), stage_f, s - AT_F)
        when(within(s - AT_A, 1, NOUT), stage_a, s - AT_A)
        when(within(s - AT_G, 0, NRET), stage_g, s - AT_G)

        when(s == AT_C, tables)
        n = s - AT_C
        when(within(n, 0, NCH), stage_c, n, 0)
        when(within(n, NCH, 2 * NCH), stage_c, n, 1)
        when(within(n, 2 * NCH, NOUT), stage_c, n, 2)

        i = s - AT_D
        for down in (False, True):
            kind = (i // NCH) % 2 == (1 if down else 0)
            kind_next = ((i + 1) // NCH) % 2 == (1 if down else 0)
            when(jnp.logical_and(within(i, 0, 4 * NCH - 1), kind_next), fetch, i + 1, down)
            now = jnp.logical_and(within(i, 0, 4 * NCH), kind)
            when(now, lambda down=down: wait((wbd if down else wbu).at[i % 2], w_sem.at[i % 2]))
        when(i == 2 * NCH, between_b)
        when(i == 3 * NCH, between_f)
        when(within(i, 2 * NCH, 3 * NCH), stage_e, i - 2 * NCH, False)
        when(within(i, 3 * NCH, 4 * NCH), stage_e, i - 2 * NCH, True)
        when(within(i, 0, NCH), stage_d, i, False, acc)
        when(within(i, NCH, 2 * NCH), stage_d, i, True, gh)
        when(within(i, 2 * NCH, NOUT), stage_d, i, False, acc)

        r = s - AT_H
        when(within(r, 0, NCH), stage_h_b, r)
        when(within(r, NCH, NRET), stage_h_f, r)
        when(r == NCH, finish_b)
        return carry

    lax.fori_loop(0, AT_H + NRET, step, 0)

    def sent(n, carry):
        wait(ag.at[0, 0, pl.ds(0, 3)], a_s.at[n])
        wait(ag.at[0, 0], b_s.at[n])
        return carry

    lax.fori_loop(0, NOUT, sent, 0)
    for n in range(NOUT - RING_S, NOUT):
        wait(snd.at[0], c_s.at[n])
    for r in range(NRET - RING_O, NRET):
        wait(ob.at[0, :, pl.ds(0, 3)], e_s.at[r])
    for r in range(NRET - RING_Z, NRET):
        wait(zb.at[0, :, 0], f_s.at[r])
    for r in range(NRET - RING_X, NRET):
        wait(xb.at[0, :, pl.ds(0, 3)], g_s.at[r])
    wait(gb, p_s.at[0])
    wait(gb, p_s.at[1])
    wait(next_f, p_r.at[0])
    wait(next_b, p_r.at[1])


def per_device(
    act_fwd, routes_fwd, mix_fwd, cot_bwd, saved_bwd, routes_bwd, mix_bwd, norm_gain, w_up, w_down
):
    vmem, far = pl.BlockSpec(memory_space=pltpu.VMEM), pl.BlockSpec(memory_space=pl.ANY)
    sems = [pltpu.SemaphoreType.DMA((NOUT,))] * 6 + [pltpu.SemaphoreType.DMA((NRET,))] * 6
    sems += [pltpu.SemaphoreType.DMA((2,))] * 5
    out = jax.ShapeDtypeStruct((ROWS, D), BF)
    next_fwd, next_bwd = pl.pallas_call(
        kernel,
        out_shape=(out, out),
        in_specs=[vmem] * 8 + [far] * 2,
        out_specs=(far, far),
        scratch_shapes=[
            pltpu.VMEM((NOUT, 2, SIDE, DEEP, ROWS, CH), BF),
            pltpu.VMEM((NOUT, 2, SIDE, SIDE, PAIR, CH), BF),
            pltpu.VMEM((RING_S, 2, SIDE - 1, SIDE, PAIR, CH), BF),
            pltpu.VMEM((2, 2, CH, HID), BF),
            pltpu.VMEM((2, 2, HID, CH), BF),
            pltpu.VMEM((RING_O, 2, SIDE, SIDE, PAIR, CH), BF),
            pltpu.VMEM((RING_Z, 2, DEEP, SIDE, ROWS, CH), BF),
            pltpu.VMEM((NRET, 2, SIDE, ROWS, CH), BF),
            pltpu.VMEM((RING_X, 2, SIDE, ROWS, CH), BF),
            pltpu.VMEM((NRET, 2, SIDE - 1, ROWS, CH), BF),
            pltpu.VMEM((NCH, 2, ROWS, CH), F32),
            pltpu.VMEM((SIDE, LINE, HID), F32),
            pltpu.VMEM((SIDE, LINE, HID), F32),
            pltpu.VMEM((SIDE, LINE, HID), BF),
            pltpu.VMEM((2, 2, SIDE, LINE, PT), BF),
            pltpu.VMEM((2, SIDE, LINE, 128), F32),
            pltpu.VMEM((2, 2, SIDE, 2 * PT, LINE), BF),
            pltpu.VMEM((2, SIDE, DEEP, ROWS, 128), F32),
            pltpu.VMEM((2, 128, 128), F32),
            pltpu.VMEM((NCH, 2, ROWS, CH), BF),
            pltpu.VMEM((ROWS, D), BF),
        ]
        + sems,
        compiler_params=pltpu.CompilerParams(
            collective_id=0, has_side_effects=True, vmem_limit_bytes=63 * 2**20
        ),
        cost_estimate=pl.CostEstimate(flops=30 * 10**9, bytes_accessed=40 * 10**6, transcendentals=2 * 10**6),
    )(
        act_fwd[0], routes_fwd[0].T, mix_fwd[0].T, cot_bwd[0], saved_bwd[0], routes_bwd[0].T, mix_bwd[0].T,
        norm_gain, w_up[0, 0], w_down[0, 0],
    )
    return next_fwd[None], next_bwd[None]


def solution(mesh):
    rows = P("pipe", "expert", None)
    return jax.shard_map(
        per_device,
        mesh=mesh,
        in_specs=(rows,) * 7 + (P("pipe", None),) + (P("pipe", "expert", None, None),) * 2,
        out_specs=(rows, rows),
        check_vma=False,
    )
```

```python
import functools

import jax
import jax.numpy as jnp
from jax import lax
from jax.experimental import pallas as pl
from jax.experimental.pallas import tpu as pltpu
from jax.sharding import PartitionSpec as P

MESH = pl.DeviceIdType.MESH
BF, F32 = jnp.bfloat16, jnp.float32

D, HID, TOP, ROWS, CAP = 3584, 1024, 8, 64, 24
SIDE, DEEP = 4, 2
HALF = D // 2
CH = 256
NCH = HALF // CH
PAIR = DEEP * CAP
LINE = SIDE * PAIR
PT = DEEP * ROWS
NOUT, NRET = 3 * NCH, 2 * NCH
RING_S, RING_O, RING_Z, RING_X = 3, 4, 7, 5
LAST = NRET - 1
AT_A, AT_B, AT_W, AT_C, AT_D = 0, 2, 3, 6, 7
AT_E = AT_D + 2 * NCH
AT_F, AT_G, AT_V, AT_H = AT_E + 2, AT_E + 5, AT_E + 7, AT_E + 11
SLOT = {0: 1, 1: 2, 2: 3, 3: 0}


def late(n):
    return n < 0


def kernel(
    act_far, routes_f, mix_f, cot_far, saved_far, routes_b, mix_b, gain, wup, wdn,
    both_next,
    act, cot, saved, i_s, xl,
    ag, rc, snd, wbu, wbd, ob, zb, zr, xb, xr, gs, acc, gh, hid, sel, scl, cw, tab, own_tab, far_tab, pair_tab, xf,
    a_s, a_r, b_s, b_r, c_s, c_r, e_s, e_r, f_s, f_r, g_s, g_r, h_s, h_r, k_s, k_r, v_s, v_r, w_sem, t_s, t_r, p_s, p_r,
):
    next_f, next_b = both_next.at[0], both_next.at[1]
    pp, me = lax.axis_index("pipe"), lax.axis_index("expert")
    z, x, y = me // (SIDE * SIDE), (me // SIDE) % SIDE, me % SIDE
    n_pipe = lax.axis_size("pipe")

    def device(dz, dx, dy):
        return (pp, ((z + dz) % DEEP) * SIDE * SIDE + ((x + dx) % SIDE) * SIDE + (y + dy) % SIDE)

    gather_at, trade_at = (x, y), (y, x)
    gather_peer = lambda v, k: device(0, k, 0) if v == 0 else device(0, 0, k)
    trade_peer = lambda v, k: device(0, 0, k) if v == 0 else device(0, k, 0)
    other = device(1, 0, 0)
    ahead, behind = ((pp + 1) % n_pipe, me), ((pp + n_pipe - 1) % n_pipe, me)
    shifts = range(1, SIDE)

    def send(src, dst, s_sem, r_sem, to):
        pltpu.make_async_remote_copy(
            src_ref=src, dst_ref=dst, send_sem=s_sem, recv_sem=r_sem, device_id=to, device_id_type=MESH
        ).start()

    def wait(ref, sem):
        pltpu.make_async_copy(ref, ref, sem).wait()

    barrier = pltpu.get_barrier_semaphore()
    peers = [other, ahead, behind] + [gather_peer(v, k) for v in range(2) for k in shifts]
    for peer in peers:
        pl.semaphore_signal(barrier, inc=1, device_id=peer, device_id_type=MESH)

    loads = [pltpu.make_async_copy(far, near, i_s.at[i]) for i, (far, near) in enumerate(((saved_far, saved), (cot_far, cot), (act_far, act)))]
    for load in loads:
        load.start()

    line = lax.broadcasted_iota(jnp.int32, (128, PT), 0)
    mine = lax.broadcasted_iota(jnp.int32, (128, PT), 1) // ROWS == z
    major, minor, field = (line // 16) % SIDE, (line // 4) % SIDE, line % 4
    is_b = field % 2 == 1
    earlier = lax.broadcasted_iota(jnp.int32, (PT, PT), 0) < lax.broadcasted_iota(jnp.int32, (PT, PT), 1)
    earlier = jnp.where(earlier, 1.0, 0.0).astype(BF)
    twice = lambda ref, k: jnp.concatenate([ref[k : k + 1, :]] * DEEP, axis=1)
    for v in range(2):
        expert_of = (line // 64) * SIDE * SIDE + (major * SIDE + minor if v == 0 else minor * SIDE + major)
        chosen = jnp.zeros((128, PT), F32)
        weight = jnp.zeros((128, PT), F32)
        for k in range(TOP):
            hit = jnp.logical_and(jnp.where(is_b, twice(routes_b, k), twice(routes_f, k)) == expert_of, mine)
            chosen = jnp.where(hit, 1.0, chosen)
            weight = jnp.where(hit, jnp.where(is_b, twice(mix_b, k), twice(mix_f, k)), weight)
        rank = jnp.dot(chosen.astype(BF), earlier, preferred_element_type=F32)
        slot = jnp.where(chosen > 0.5, rank + (z * CAP + 1).astype(F32), 0.0)
        table = jnp.where(field < 2, slot, weight)
        for zz in range(DEEP):
            own_tab[v, zz] = table[zz * 64 : (zz + 1) * 64].reshape(SIDE, 16, PT)

    def spread(array, wide):
        for v in range(2):
            for j in range(NCH):
                lo = v * HALF + j * CH
                ag[array * NCH + j, v, 1, z] = wide[:, lo : lo + CH].astype(BF)

    def normed(ref):
        wide = ref[...].astype(F32)
        recip = lax.rsqrt(jnp.sum(wide * wide, axis=-1, keepdims=True) * (1.0 / D) + 1e-06)
        return wide * recip, recip

    loads[0].wait()
    spread(0, normed(saved)[0] * gain[...])

    def choose(n, early, after):
        pl.when(late(n))(after)
        pl.when(jnp.logical_not(late(n)))(early)

    top, bottom = pl.ds(0, ROWS // 2), pl.ds(ROWS // 2, ROWS // 2)

    def stage_a(n):
        for v in range(2):
            own = ag.at[n, v, 1, z]
            send(own, ag.at[n, v, 0, z], a_s.at[n], a_r.at[n], gather_peer(v, 1))
            send(own, ag.at[n, v, 2, z], a_s.at[n], a_r.at[n], gather_peer(v, 3))

    def stage_b(n):
        wait(ag.at[n, 0, pl.ds(0, 2)], a_r.at[n])
        for v in range(2):
            part = ag.at[n, v, pl.ds(0, 3), z]
            send(part, part, b_s.at[n], b_r.at[n], other)

        @pl.when(jnp.logical_not(late(n)))
        def _():
            for v in range(2):
                send(ag.at[n, v, 0, z, top], ag.at[n, v, 3, z, top], h_s.at[n], h_r.at[n], gather_peer(v, 1))
                send(ag.at[n, v, 2, z, bottom], ag.at[n, v, 3, z, bottom], h_s.at[n], h_r.at[n], gather_peer(v, 3))

    def stage_w(n):
        def early():
            wait(ag.at[n, :, 3, 0], h_r.at[n])
            for v in range(2):
                send(ag.at[n, v, 3, z], ag.at[n, v, 3, z], k_s.at[n], k_r.at[n], other)

        def after():
            wait(ag.at[n, :, pl.ds(0, 3), 0], b_r.at[n])
            for v in range(2):
                send(ag.at[n, v, 0, :, top], ag.at[n, v, 3, :, top], h_s.at[n], h_r.at[n], gather_peer(v, 1))
                send(ag.at[n, v, 2, :, bottom], ag.at[n, v, 3, :, bottom], h_s.at[n], h_r.at[n], gather_peer(v, 3))

        choose(n, early, after)

    def gathered(n):
        def early():
            wait(ag.at[n, :, pl.ds(0, 3), 0], b_r.at[n])
            wait(ag.at[n, :, 3, 0], k_r.at[n])

        choose(n, early, lambda: wait(ag.at[n, :, 3], h_r.at[n]))

    def first_a():
        for v in range(2):
            own = ag.at[0, v, 1, z]
            send(own, own, a_s.at[0], a_r.at[0], other)

    def first_b():
        wait(ag.at[0, 0, 0], a_r.at[0])
        for v in range(2):
            for k in shifts:
                send(ag.at[0, v, 1], ag.at[0, v, SLOT[SIDE - k]], b_s.at[0], b_r.at[0], gather_peer(v, k))

    def stage_c(n, array):
        batch = 1 if array < 2 else 0
        ring = n % RING_S
        if array == 0:
            pl.when(n == 0)(lambda: wait(ag.at[0, :, pl.ds(0, 3)], b_r.at[0]))
            pl.when(n > 0)(lambda: gathered(n))
        else:
            gathered(n)

        @pl.when(n >= RING_S)
        def _():
            wait(snd.at[ring], c_s.at[n - RING_S])

        def one(i, carry):
            for v in range(2):
                q = (gather_at[v] + i + SIDE - 1) % SIDE
                rows = ag[n, v, i].reshape(PT, CH)
                got = jnp.dot(sel[batch, v, i], rows, preferred_element_type=F32)
                if array == 1:
                    got = got * scl[v, i][:, 0:1]
                got = got.astype(BF).reshape(SIDE, PAIR, CH)
                if v == 0:
                    rc[n, 0, q, y] = got[0]
                else:
                    rc[n, 1, x, q] = got[0]
                for d in shifts:
                    snd[ring, v, d - 1, q] = got[d]
            return carry

        lax.fori_loop(0, SIDE, one, 0)
        for k in shifts:
            send(snd.at[ring, 0, k - 1], rc.at[n, 0, :, y], c_s.at[n], c_r.at[n], trade_peer(0, k))
            send(snd.at[ring, 1, k - 1], rc.at[n, 1, x], c_s.at[n], c_r.at[n], trade_peer(1, k))

    def fetch(i, down):
        j, ring = i % NCH, i % 2
        for v in range(2):
            cols = pl.ds(pl.multiple_of(v * HALF + j * CH, CH), CH)
            if down:
                pltpu.make_async_copy(wdn.at[:, cols], wbd.at[ring, v], w_sem.at[ring]).start()
            else:
                pltpu.make_async_copy(wup.at[cols, :], wbu.at[ring, v], w_sem.at[ring]).start()

    NT = (((1,), (1,)), ((), ()))

    def stage_d(n, down, total):
        ring = n % 2
        six = rc.at[n, :, pl.ds(0, 3)]
        wait(six, c_r.at[n])

        def one(q, carry):
            out = total[q]
            for v in range(2):
                rows = rc[n, v, q].reshape(LINE, CH)
                if down:
                    out = out + lax.dot_general(rows, wbd[ring, v], NT, preferred_element_type=F32)
                else:
                    out = out + jnp.dot(rows, wbu[ring, v], preferred_element_type=F32)
            total[q] = out
            return carry

        lax.fori_loop(0, SIDE, one, 0)

    def stage_e(r, down):
        ring, wring = r % RING_O, r % 2

        @pl.when(r >= RING_O)
        def _():
            wait(ob.at[ring, :, pl.ds(0, 3)], e_s.at[r - RING_O])

        def one(q, carry):
            for v in range(2):
                if down:
                    got = jnp.dot(hid[q], wbd[wring, v], preferred_element_type=F32)
                else:
                    got = lax.dot_general(hid[q], wbu[wring, v], NT, preferred_element_type=F32)
                ob[ring, v, q] = got.astype(BF).reshape(SIDE, PAIR, CH)
            return carry

        lax.fori_loop(0, SIDE, one, 0)
        for k in shifts:
            send(ob.at[ring, 0, :, (y + k) % SIDE], rc.at[r, 0, SIDE - k], e_s.at[r], e_r.at[r], trade_peer(0, k))
            send(ob.at[ring, 1, (x + k) % SIDE], rc.at[r, 1, SIDE - k], e_s.at[r], e_r.at[r], trade_peer(1, k))
        for q in range(SIDE):
            rc[r, 0, 0, q] = ob[ring, 0, q, y]
        rc[r, 1, 0] = ob[ring, 1, x]

    def combine(r):
        ring = r % RING_Z
        unit = r // NCH
        wait(rc.at[r, :, pl.ds(1, 3)], e_r.at[r])

        @pl.when(r >= RING_Z)
        def _():
            sent_back(r - RING_Z)

        def one(i, carry):
            for v in range(2):
                q = (gather_at[v] + i + SIDE - 1) % SIDE
                rows = rc[r, v, :, q].reshape(LINE, CH)
                both = jnp.dot(cw[unit, v, i], rows, preferred_element_type=F32)
                part = (both[:PT] + both[PT:]).astype(BF).reshape(DEEP, ROWS, CH)
                for zz in range(DEEP):
                    zb[ring, v, zz, i] = part[zz]
            return carry

        lax.fori_loop(0, SIDE, one, 0)

    def sent_back(r):
        def early():
            wait(zb.at[0, :, 0], f_s.at[r])

        def after():
            wait(zb.at[0, :, :, 3], v_s.at[r])
            wait(zb.at[0, :, 0, pl.ds(0, 3)], f_s.at[r])

        choose(r, early, after)

    def stage_f(r):
        combine(r)
        ring = r % RING_Z

        def early():
            for v in range(2):
                send(zb.at[ring, v, 1 - z], zr.at[r, v], f_s.at[r], f_r.at[r], other)

        def after():
            for v in range(2):
                send(zb.at[ring, v, :, 3, top], xf.at[r, v, 0], v_s.at[r], v_r.at[r], gather_peer(v, 1))
                send(zb.at[ring, v, :, 3, bottom], xf.at[r, v, 1], v_s.at[r], v_r.at[r], gather_peer(v, 3))

        choose(r, early, after)

    def stage_g(r):
        ring, xring = r % RING_Z, r % RING_X

        @pl.when(r >= RING_X)
        def _():
            wait(xb.at[0, :, pl.ds(0, 2)], g_s.at[r - RING_X])
            pl.when(jnp.logical_not(late(r - RING_X)))(lambda: wait(xb.at[0, :, 0], v_s.at[r - RING_X]))

        def early():
            wait(zr.at[r], f_r.at[r])
            for v in range(2):
                xb[xring, v, 3] = (zb[ring, v, z, 3].astype(F32) + zr[r, v, 3].astype(F32)).astype(BF)
                send(xb.at[xring, v, 3, top], xf.at[r, v, 0, 0], v_s.at[r], v_r.at[r], gather_peer(v, 1))
                send(xb.at[xring, v, 3, bottom], xf.at[r, v, 1, 0], v_s.at[r], v_r.at[r], gather_peer(v, 3))

        def after():
            wait(xf.at[r], v_r.at[r])
            for v in range(2):
                for zz in range(DEEP):
                    zb[ring, v, zz, 2, top] = (zb[ring, v, zz, 2, top].astype(F32) + xf[r, v, 0, zz].astype(F32)).astype(BF)
                    zb[ring, v, zz, 0, bottom] = (zb[ring, v, zz, 0, bottom].astype(F32) + xf[r, v, 1, zz].astype(F32)).astype(BF)
                part = pl.ds(0, 3)
                send(zb.at[ring, v, 1 - z, part], zr.at[r, v, part], f_s.at[r], f_r.at[r], other)

        choose(r, early, after)

    def stage_v(r):
        ring, xring = r % RING_Z, r % RING_X
        choose(r, lambda: wait(xf.at[r, :, :, 0], v_r.at[r]), lambda: wait(zr.at[r, :, pl.ds(0, 3)], f_r.at[r]))
        for v in range(2):
            for i in range(3):
                xb[xring, v, i] = (zb[ring, v, z, i].astype(F32) + zr[r, v, i].astype(F32)).astype(BF)

            @pl.when(jnp.logical_not(late(r)))
            def _():
                for i, rows, j in ((2, top, 0), (0, bottom, 1)):
                    xb[xring, v, i, rows] = (
                        zb[ring, v, z, i, rows].astype(F32) + zr[r, v, i, rows].astype(F32) + xf[r, v, j, 0].astype(F32)
                    ).astype(BF)

            send(xb.at[xring, v, 2], xr.at[r, v, 0], g_s.at[r], g_r.at[r], gather_peer(v, 1))
            send(xb.at[xring, v, 0], xr.at[r, v, 1], g_s.at[r], g_r.at[r], gather_peer(v, 3))

    xz = wbu.at[0]
    half = lambda zz: pl.ds(pl.multiple_of(zz * ROWS, ROWS), ROWS)

    def last_f():
        combine(LAST)
        for v in range(2):
            for k in shifts:
                part = zb.at[LAST % RING_Z, v, :, SLOT[k]]
                send(part, xl.at[v, k - 1], f_s.at[LAST], f_r.at[LAST], gather_peer(v, k))

    def last_g():
        wait(xl, f_r.at[LAST])
        for v in range(2):
            for zz in range(DEEP):
                out = zb[LAST % RING_Z, v, zz, 1].astype(F32)
                for k in range(SIDE - 1):
                    out = out + xl[v, k, zz].astype(F32)
                xz[v, zz * ROWS : (zz + 1) * ROWS, :CH] = out.astype(BF)
            send(xz.at[v, half(1 - z), pl.ds(0, CH)], xr.at[LAST, v, 0], g_s.at[LAST], g_r.at[LAST], other)

    def summed(r, v):
        return xb[r % RING_X, v, 1].astype(F32) + xr[r, v, 0].astype(F32) + xr[r, v, 1].astype(F32)

    def stage_h_b(r):
        wait(xr.at[r], g_r.at[r])
        for v in range(2):
            gs[r, v] = summed(r, v)

    def last_sum(r, v):
        return xz[v, half(z), :CH].astype(F32) + xr[LAST, v, 0].astype(F32)

    def stage_h_f(r, total=summed):
        if total is summed:
            wait(xr.at[r], g_r.at[r])
        else:
            wait(xr.at[LAST, :, 0], g_r.at[LAST])
        j = r - NCH
        for v in range(2):
            cols = pl.ds(pl.multiple_of(v * HALF + j * CH, CH), CH)
            act[:, cols] = (act[:, cols].astype(F32) + total(r, v)).astype(BF)
            send(act.at[:, cols], next_f.at[:, cols], p_s.at[0], p_r.at[0], ahead)

    def finish_b():
        scaled, recip = normed(saved)
        total = jnp.zeros((ROWS, 1), F32)
        parts = []
        for v in range(2):
            for j in range(NCH):
                lo = v * HALF + j * CH
                g_n = gs[j, v] * gain[:, lo : lo + CH]
                gs[j, v] = g_n
                total = total + jnp.sum(g_n * scaled[:, lo : lo + CH], axis=-1, keepdims=True)
        mean = total * (1.0 / D)
        for v in range(2):
            for j in range(NCH):
                lo = v * HALF + j * CH
                g_x = recip * (gs[j, v] - scaled[:, lo : lo + CH] * mean)
                cot[:, lo : lo + CH] = (cot[:, lo : lo + CH].astype(F32) + g_x).astype(BF)
        send(cot, next_b, p_s.at[1], p_r.at[1], behind)

    def when(condition, stage, *args):
        pl.when(condition)(lambda: stage(*args))

    def within(i, lo, hi):
        return jnp.logical_and(i >= lo, i < hi)

    pl.semaphore_wait(barrier, len(peers))
    first_a()
    send(own_tab.at[:, 1 - z], far_tab, t_s.at[0], t_r.at[0], other)
    stage_a(1)
    fetch(0, False)
    first_b()
    wait(far_tab, t_r.at[0])
    for v in range(2):
        pair_tab[v] = own_tab[v, z] + far_tab[v]
        tab[v, 1] = pair_tab[v, gather_at[v]]
        for k in shifts:
            part = pair_tab.at[v, (gather_at[v] + k) % SIDE]
            send(part, tab.at[v, SLOT[SIDE - k]], t_s.at[1], t_r.at[1], gather_peer(v, k))

    slot_row = lax.broadcasted_iota(jnp.int32, (PAIR, 128), 0).astype(F32) + 1.0
    def trade_row(v, d, field):
        return pl.ds(((trade_at[v] + d) % SIDE) * 4 + field, 1)

    def pick_tables(batch):
        def one(i, carry):
            for v in range(2):
                for d in range(SIDE):
                    hit = tab[v, i, trade_row(v, d, batch), :] == slot_row
                    sel[batch, v, i, d * PAIR : (d + 1) * PAIR, :] = jnp.where(hit, 1.0, 0.0).astype(BF)
            return carry

        lax.fori_loop(0, SIDE, one, 0)

    def scale_tables():
        def one(i, carry):
            for v in range(2):
                for d in range(SIDE):
                    gate = tab[v, i, trade_row(v, d, 3), :]
                    picked = sel[1, v, i, d * PAIR : (d + 1) * PAIR, :].astype(F32) * gate
                    scl[v, i, d * PAIR : (d + 1) * PAIR, :] = jnp.broadcast_to(
                        jnp.sum(picked, axis=1, keepdims=True), (PAIR, 128)
                    )
            return carry

        lax.fori_loop(0, SIDE, one, 0)

    def sum_tables(i):
        rest = jnp.zeros((2 * PT - LINE, PT), F32)
        for v in range(2):
            ones, gates = [], []
            for d in range(SIDE):
                ones.append(jnp.where(tab[v, i, trade_row(v, d, 1), :] == slot_row, 1.0, 0.0))
                hit = tab[v, i, trade_row(v, d, 0), :] == slot_row
                gates.append(jnp.where(hit, tab[v, i, trade_row(v, d, 2), :], 0.0))
            gate = jnp.concatenate(gates + [rest], axis=0).T[:, :LINE]
            one = jnp.concatenate(ones + [rest], axis=0).T[:, :LINE]
            high = gate.astype(BF)
            cw[1, v, i, :PT] = high
            cw[1, v, i, PT:] = (gate - high.astype(F32)).astype(BF)
            cw[0, v, i, :PT] = one.astype(BF)
            cw[0, v, i, PT:] = jnp.zeros((PT, LINE), BF)

    def tables():
        wait(tab.at[:, pl.ds(0, 3)], t_r.at[1])
        pick_tables(1)

    def load_cot():
        loads[1].wait()
        spread(1, cot[...])

    def load_act():
        loads[2].wait()
        spread(2, normed(act)[0] * gain[...])

    def clear():
        acc[...] = jnp.zeros_like(acc)
        gh[...] = jnp.zeros_like(gh)

    def between_b():
        def one(q, carry):
            p = acc[q]
            sigma = jax.nn.sigmoid(p)
            hid[q] = (gh[q] * sigma * (1.0 + p * (1.0 - sigma))).astype(BF)
            acc[q] = jnp.zeros_like(p)
            return carry

        lax.fori_loop(0, SIDE, one, 0)

    def between_f():
        def one(q, carry):
            p = acc[q]
            hid[q] = (p * jax.nn.sigmoid(p)).astype(BF)
            return carry

        lax.fori_loop(0, SIDE, one, 0)

    def step(s, carry):
        when(within(s - AT_B, 1, NOUT), stage_b, s - AT_B)
        when(within(s - AT_F, 0, LAST), stage_f, s - AT_F)
        when(s - AT_F == LAST, last_f)
        when(within(s - AT_W, 1, NOUT), stage_w, s - AT_W)
        when(within(s - AT_A, 2, NOUT), stage_a, s - AT_A)
        when(within(s - AT_V, 0, LAST), stage_v, s - AT_V)
        when(within(s - AT_G, 0, LAST), stage_g, s - AT_G)
        when(s - AT_G == LAST, last_g)

        when(s == AT_C, tables)
        n = s - AT_C
        when(within(n, 0, NCH), stage_c, n, 0)
        when(within(n, NCH, 2 * NCH), stage_c, n, 1)
        when(within(n, 2 * NCH, NOUT), stage_c, n, 2)

        i = s - AT_D
        for down in (False, True):
            kind = (i // NCH) % 2 == (1 if down else 0)
            kind_next = ((i + 1) // NCH) % 2 == (1 if down else 0)
            when(jnp.logical_and(within(i, 0, 4 * NCH - 1), kind_next), fetch, i + 1, down)
            now = jnp.logical_and(within(i, 0, 4 * NCH), kind)
            when(now, lambda down=down: wait((wbd if down else wbu).at[i % 2], w_sem.at[i % 2]))
        when(i == 2 * NCH, between_b)
        when(i == 3 * NCH, between_f)
        when(within(i, 2 * NCH, 3 * NCH), stage_e, i - 2 * NCH, False)
        when(within(i, 3 * NCH, 4 * NCH), stage_e, i - 2 * NCH, True)
        when(within(i, 0, NCH), stage_d, i, False, acc)
        when(within(i, NCH, 2 * NCH), stage_d, i, True, gh)
        when(within(i, 2 * NCH, NOUT), stage_d, i, False, acc)

        r = s - AT_H
        when(within(r, 0, NCH), stage_h_b, r)
        when(within(r, NCH, LAST), stage_h_f, r)
        when(r == LAST, stage_h_f, LAST, last_sum)
        when(r == NCH, finish_b)

        when(s == AT_C - 2, clear)
        when(s == AT_C - 1, load_cot)
        when(s == AT_C + 2, scale_tables)
        when(s == AT_C + 3, load_act)
        when(s == AT_C + 4, pick_tables, 0)
        when(within(s - (AT_C + 5), 0, SIDE), sum_tables, s - (AT_C + 5))
        return carry

    lax.fori_loop(0, AT_H + NRET, step, 0)

    def sent(n, carry):
        wait(ag.at[0, 0, pl.ds(0, 2)], a_s.at[n])
        wait(ag.at[0, :, pl.ds(0, 3), 0], b_s.at[n])

        def early():
            wait(ag.at[0, :, 3, 0], h_s.at[n])
            wait(ag.at[0, :, 3, 0], k_s.at[n])

        choose(n, early, lambda: wait(ag.at[0, :, 3], h_s.at[n]))
        return carry

    lax.fori_loop(1, NOUT, sent, 0)
    wait(ag.at[0, 0, 0], a_s.at[0])
    wait(ag.at[0, :, pl.ds(0, 3)], b_s.at[0])
    wait(far_tab, t_s.at[0])
    wait(tab.at[:, pl.ds(0, 3)], t_s.at[1])
    for n in range(NOUT - RING_S, NOUT):
        wait(snd.at[0], c_s.at[n])
    for r in range(NRET - RING_O, NRET):
        wait(ob.at[0, :, pl.ds(0, 3)], e_s.at[r])
    for r in range(NRET - RING_Z, LAST):
        if late(r):
            wait(zb.at[0, :, :, 3], v_s.at[r])
            wait(zb.at[0, :, 0, pl.ds(0, 3)], f_s.at[r])
        else:
            wait(zb.at[0, :, 0], f_s.at[r])
    wait(xl, f_s.at[LAST])
    for r in range(LAST - RING_X, LAST):
        wait(xb.at[0, :, pl.ds(0, 2)], g_s.at[r])
        if not late(r):
            wait(xb.at[0, :, 0], v_s.at[r])
    wait(xr.at[0, :, 0], g_s.at[LAST])
    wait(cot, p_s.at[0])
    wait(cot, p_s.at[1])
    wait(next_f, p_r.at[0])
    wait(next_b, p_r.at[1])


def per_device(
    act_fwd, routes_fwd, mix_fwd, cot_bwd, saved_bwd, routes_bwd, mix_bwd, norm_gain, w_up, w_down
):
    vmem, far = pl.BlockSpec(memory_space=pltpu.VMEM), pl.BlockSpec(memory_space=pl.ANY)
    sems = [pltpu.SemaphoreType.DMA((NOUT,))] * 6 + [pltpu.SemaphoreType.DMA((NRET,))] * 6
    sems += [pltpu.SemaphoreType.DMA((NOUT,))] * 4 + [pltpu.SemaphoreType.DMA((NRET,))] * 2
    sems += [pltpu.SemaphoreType.DMA((2,))] * 5
    out = jax.ShapeDtypeStruct((2, ROWS, D), BF)
    both = pl.pallas_call(
        kernel,
        out_shape=out,
        in_specs=[far, vmem, vmem, far, far, vmem, vmem, vmem, far, far],
        out_specs=far,
        scratch_shapes=[
            pltpu.VMEM((ROWS, D), BF),
            pltpu.VMEM((ROWS, D), BF),
            pltpu.VMEM((ROWS, D), BF),
            pltpu.SemaphoreType.DMA((3,)),
            pltpu.VMEM((2, SIDE - 1, DEEP, ROWS, CH), BF),
            pltpu.VMEM((NOUT, 2, SIDE, DEEP, ROWS, CH), BF),
            pltpu.VMEM((NOUT, 2, SIDE, SIDE, PAIR, CH), BF),
            pltpu.VMEM((RING_S, 2, SIDE - 1, SIDE, PAIR, CH), BF),
            pltpu.VMEM((2, 2, CH, HID), BF),
            pltpu.VMEM((2, 2, HID, CH), BF),
            pltpu.VMEM((RING_O, 2, SIDE, SIDE, PAIR, CH), BF),
            pltpu.VMEM((RING_Z, 2, DEEP, SIDE, ROWS, CH), BF),
            pltpu.VMEM((NRET, 2, SIDE, ROWS, CH), BF),
            pltpu.VMEM((RING_X, 2, SIDE, ROWS, CH), BF),
            pltpu.VMEM((NRET, 2, 2, ROWS, CH), BF),
            pltpu.VMEM((NCH, 2, ROWS, CH), F32),
            pltpu.VMEM((SIDE, LINE, HID), F32),
            pltpu.VMEM((SIDE, LINE, HID), F32),
            pltpu.VMEM((SIDE, LINE, HID), BF),
            pltpu.VMEM((2, 2, SIDE, LINE, PT), BF),
            pltpu.VMEM((2, SIDE, LINE, 128), F32),
            pltpu.VMEM((2, 2, SIDE, 2 * PT, LINE), BF),
            pltpu.VMEM((2, SIDE, 16, PT), F32),
            pltpu.VMEM((2, DEEP, SIDE, 16, PT), F32),
            pltpu.VMEM((2, SIDE, 16, PT), F32),
            pltpu.VMEM((2, SIDE, 16, PT), F32),
            pltpu.VMEM((NRET, 2, 2, DEEP, ROWS // 2, CH), BF),
        ]
        + sems,
        compiler_params=pltpu.CompilerParams(
            collective_id=0, has_side_effects=True, vmem_limit_bytes=63 * 2**20
        ),
        cost_estimate=pl.CostEstimate(flops=30 * 10**9, bytes_accessed=40 * 10**6, transcendentals=2 * 10**6),
    )(
        act_fwd[0], routes_fwd[0].T, mix_fwd[0].T, cot_bwd[0], saved_bwd[0], routes_bwd[0].T, mix_bwd[0].T,
        norm_gain, w_up[0, 0], w_down[0, 0],
    )
    return both[0:1], both[1:2]


def solution(mesh):
    rows = P("pipe", "expert", None)
    return jax.shard_map(
        per_device,
        mesh=mesh,
        in_specs=(rows,) * 7 + (P("pipe", None),) + (P("pipe", "expert", None, None),) * 2,
        out_specs=(rows, rows),
        check_vma=False,
    )
```

```python
import functools

import jax
import jax.numpy as jnp
from jax import lax
from jax.experimental import pallas as pl
from jax.experimental.pallas import tpu as pltpu
from jax.sharding import PartitionSpec as P

MESH = pl.DeviceIdType.MESH
BF, F32 = jnp.bfloat16, jnp.float32

D, HID, TOP, ROWS, CAP = 3584, 1024, 8, 64, 24
SIDE, DEEP = 4, 2
HALF = D // 2
CH = 256
NCH = HALF // CH
PAIR = DEEP * CAP
LINE = SIDE * PAIR
PT = DEEP * ROWS
NOUT, NRET = 3 * NCH, 2 * NCH
RING_S, RING_O, RING_Z, RING_X = 3, 4, 7, 5
LAST = NRET - 1
AT_A, AT_B, AT_W, AT_C, AT_D = 0, 6, 7, 8, 11
AT_E = AT_D + 2 * NCH
AT_F, AT_G, AT_V, AT_H = AT_E + 4, AT_E + 7, AT_E + 10, AT_E + 13
SLOT = {0: 1, 1: 2, 2: 3, 3: 0}


LATE_OUT, LATE_BACK = (1, 2, 10, 11, 12, 13, 15, 16), (5, 8, 11)


def among(n, chunks):
    found = n == chunks[0]
    for one in chunks[1:]:
        found = jnp.logical_or(found, n == one)
    return found


def kernel(
    act_far, routes_f, mix_f, cot_far, saved_far, routes_b, mix_b, gain, wup, wdn,
    both_next,
    act, cot, saved, i_s, xl,
    ag, rc, snd, wbu, wbd, ob, zb, zr, xb, xr, gs, acc, gh, hid, sel, scl, cw, tab, own_tab, far_tab, pair_tab, xf,
    a_s, a_r, b_s, b_r, c_s, c_r, e_s, e_r, f_s, f_r, g_s, g_r, h_s, h_r, k_s, k_r, v_s, v_r, w_sem, t_s, t_r, p_s, p_r,
):
    next_f, next_b = both_next.at[0], both_next.at[1]
    pp, me = lax.axis_index("pipe"), lax.axis_index("expert")
    z, x, y = me // (SIDE * SIDE), (me // SIDE) % SIDE, me % SIDE
    n_pipe = lax.axis_size("pipe")

    def device(dz, dx, dy):
        return (pp, ((z + dz) % DEEP) * SIDE * SIDE + ((x + dx) % SIDE) * SIDE + (y + dy) % SIDE)

    gather_at, trade_at = (x, y), (y, x)
    gather_peer = lambda v, k: device(0, k, 0) if v == 0 else device(0, 0, k)
    trade_peer = lambda v, k: device(0, 0, k) if v == 0 else device(0, k, 0)
    other = device(1, 0, 0)
    ahead, behind = ((pp + 1) % n_pipe, me), ((pp + n_pipe - 1) % n_pipe, me)
    shifts = range(1, SIDE)

    def send(src, dst, s_sem, r_sem, to):
        pltpu.make_async_remote_copy(
            src_ref=src, dst_ref=dst, send_sem=s_sem, recv_sem=r_sem, device_id=to, device_id_type=MESH
        ).start()

    def wait(ref, sem):
        pltpu.make_async_copy(ref, ref, sem).wait()

    barrier = pltpu.get_barrier_semaphore()
    other_ahead, other_behind = (ahead[0], other[1]), (behind[0], other[1])
    peers = [other, ahead, behind, other_behind] + [gather_peer(v, k) for v in range(2) for k in shifts]
    for peer in peers:
        pl.semaphore_signal(barrier, inc=1, device_id=peer, device_id_type=MESH)

    loads = [pltpu.make_async_copy(far, near, i_s.at[i]) for i, (far, near) in enumerate(((saved_far, saved), (cot_far, cot), (act_far, act)))]
    for load in loads:
        load.start()

    line = lax.broadcasted_iota(jnp.int32, (128, PT), 0)
    mine = lax.broadcasted_iota(jnp.int32, (128, PT), 1) // ROWS == z
    major, minor, field = (line // 16) % SIDE, (line // 4) % SIDE, line % 4
    is_b = field % 2 == 1
    earlier = lax.broadcasted_iota(jnp.int32, (PT, PT), 0) < lax.broadcasted_iota(jnp.int32, (PT, PT), 1)
    earlier = jnp.where(earlier, 1.0, 0.0).astype(BF)
    twice = lambda ref, k: jnp.concatenate([ref[k : k + 1, :]] * DEEP, axis=1)
    for v in range(2):
        expert_of = (line // 64) * SIDE * SIDE + (major * SIDE + minor if v == 0 else minor * SIDE + major)
        chosen = jnp.zeros((128, PT), F32)
        weight = jnp.zeros((128, PT), F32)
        for k in range(TOP):
            hit = jnp.logical_and(jnp.where(is_b, twice(routes_b, k), twice(routes_f, k)) == expert_of, mine)
            chosen = jnp.where(hit, 1.0, chosen)
            weight = jnp.where(hit, jnp.where(is_b, twice(mix_b, k), twice(mix_f, k)), weight)
        rank = jnp.dot(chosen.astype(BF), earlier, preferred_element_type=F32)
        slot = jnp.where(chosen > 0.5, rank + (z * CAP + 1).astype(F32), 0.0)
        table = jnp.where(field < 2, slot, weight)
        for zz in range(DEEP):
            own_tab[v, zz] = table[zz * 64 : (zz + 1) * 64].reshape(SIDE, 16, PT)

    def spread(array, wide):
        for v in range(2):
            for j in range(NCH):
                lo = v * HALF + j * CH
                ag[array * NCH + j, v, 1, z] = wide[:, lo : lo + CH].astype(BF)

    def normed(ref):
        wide = ref[...].astype(F32)
        recip = lax.rsqrt(jnp.sum(wide * wide, axis=-1, keepdims=True) * (1.0 / D) + 1e-06)
        return wide * recip, recip

    loads[0].wait()
    spread(0, normed(saved)[0] * gain[...])

    def choose(late, early, after):
        pl.when(late)(after)
        pl.when(jnp.logical_not(late))(early)

    late_out, late_back = (lambda n: among(n, LATE_OUT)), (lambda r: among(r, LATE_BACK))

    top, bottom = pl.ds(0, ROWS // 2), pl.ds(ROWS // 2, ROWS // 2)

    def stage_a(n):
        for v in range(2):
            own = ag.at[n, v, 1, z]
            send(own, ag.at[n, v, 0, z], a_s.at[n], a_r.at[n], gather_peer(v, 1))
            send(own, ag.at[n, v, 2, z], a_s.at[n], a_r.at[n], gather_peer(v, 3))

    def stage_b(n):
        wait(ag.at[n, 0, pl.ds(0, 2)], a_r.at[n])
        for v in range(2):
            part = ag.at[n, v, pl.ds(0, 3), z]
            send(part, part, b_s.at[n], b_r.at[n], other)

        @pl.when(jnp.logical_not(late_out(n)))
        def _():
            for v in range(2):
                send(ag.at[n, v, 0, z, top], ag.at[n, v, 3, z, top], h_s.at[n], h_r.at[n], gather_peer(v, 1))
                send(ag.at[n, v, 2, z, bottom], ag.at[n, v, 3, z, bottom], h_s.at[n], h_r.at[n], gather_peer(v, 3))

    def stage_w(n):
        def early():
            wait(ag.at[n, :, 3, 0], h_r.at[n])
            for v in range(2):
                send(ag.at[n, v, 3, z], ag.at[n, v, 3, z], k_s.at[n], k_r.at[n], other)

        def after():
            wait(ag.at[n, :, pl.ds(0, 3), 0], b_r.at[n])
            for v in range(2):
                send(ag.at[n, v, 0, :, top], ag.at[n, v, 3, :, top], h_s.at[n], h_r.at[n], gather_peer(v, 1))
                send(ag.at[n, v, 2, :, bottom], ag.at[n, v, 3, :, bottom], h_s.at[n], h_r.at[n], gather_peer(v, 3))

        choose(late_out(n), early, after)

    def gathered(n):
        def early():
            wait(ag.at[n, :, pl.ds(0, 3), 0], b_r.at[n])
            wait(ag.at[n, :, 3, 0], k_r.at[n])

        choose(late_out(n), early, lambda: wait(ag.at[n, :, 3], h_r.at[n]))

    def first_a():
        for v in range(2):
            own = ag.at[0, v, 1, z]
            send(own, own, a_s.at[0], a_r.at[0], other)

    def first_b():
        wait(ag.at[0, 0, 0], a_r.at[0])
        for v in range(2):
            for k in shifts:
                send(ag.at[0, v, 1], ag.at[0, v, SLOT[SIDE - k]], b_s.at[0], b_r.at[0], gather_peer(v, k))

    def stage_c(n, array):
        batch = 1 if array < 2 else 0
        ring = n % RING_S
        if array == 0:
            pl.when(n == 0)(lambda: wait(ag.at[0, :, pl.ds(0, 3)], b_r.at[0]))
            pl.when(n > 0)(lambda: gathered(n))
        else:
            gathered(n)

        @pl.when(n >= RING_S)
        def _():
            wait(snd.at[ring], c_s.at[n - RING_S])

        def one(i, carry):
            for v in range(2):
                q = (gather_at[v] + i + SIDE - 1) % SIDE
                rows = ag[n, v, i].reshape(PT, CH)
                got = jnp.dot(sel[batch, v, i], rows, preferred_element_type=F32)
                if array == 1:
                    got = got * scl[v, i][:, 0:1]
                got = got.astype(BF).reshape(SIDE, PAIR, CH)
                if v == 0:
                    rc[n, 0, q, y] = got[0]
                else:
                    rc[n, 1, x, q] = got[0]
                for d in shifts:
                    snd[ring, v, d - 1, q] = got[d]
            return carry

        lax.fori_loop(0, SIDE, one, 0)
        for k in shifts:
            send(snd.at[ring, 0, k - 1], rc.at[n, 0, :, y], c_s.at[n], c_r.at[n], trade_peer(0, k))
            send(snd.at[ring, 1, k - 1], rc.at[n, 1, x], c_s.at[n], c_r.at[n], trade_peer(1, k))

    def fetch(i, down):
        j, ring = i % NCH, i % 2
        for v in range(2):
            cols = pl.ds(pl.multiple_of(v * HALF + j * CH, CH), CH)
            if down:
                pltpu.make_async_copy(wdn.at[:, cols], wbd.at[ring, v], w_sem.at[ring]).start()
            else:
                pltpu.make_async_copy(wup.at[cols, :], wbu.at[ring, v], w_sem.at[ring]).start()

    NT = (((1,), (1,)), ((), ()))

    def stage_d(n, down, total):
        ring = n % 2
        six = rc.at[n, :, pl.ds(0, 3)]
        wait(six, c_r.at[n])

        def one(q, carry):
            out = total[q]
            for v in range(2):
                rows = rc[n, v, q].reshape(LINE, CH)
                if down:
                    out = out + lax.dot_general(rows, wbd[ring, v], NT, preferred_element_type=F32)
                else:
                    out = out + jnp.dot(rows, wbu[ring, v], preferred_element_type=F32)
            total[q] = out
            return carry

        lax.fori_loop(0, SIDE, one, 0)

    def stage_e(r, down):
        ring, wring = r % RING_O, r % 2

        @pl.when(r >= RING_O)
        def _():
            wait(ob.at[ring, :, pl.ds(0, 3)], e_s.at[r - RING_O])

        def one(q, carry):
            for v in range(2):
                if down:
                    got = jnp.dot(hid[q], wbd[wring, v], preferred_element_type=F32)
                else:
                    got = lax.dot_general(hid[q], wbu[wring, v], NT, preferred_element_type=F32)
                ob[ring, v, q] = got.astype(BF).reshape(SIDE, PAIR, CH)
            return carry

        lax.fori_loop(0, SIDE, one, 0)
        for k in shifts:
            send(ob.at[ring, 0, :, (y + k) % SIDE], rc.at[r, 0, SIDE - k], e_s.at[r], e_r.at[r], trade_peer(0, k))
            send(ob.at[ring, 1, (x + k) % SIDE], rc.at[r, 1, SIDE - k], e_s.at[r], e_r.at[r], trade_peer(1, k))
        for q in range(SIDE):
            rc[r, 0, 0, q] = ob[ring, 0, q, y]
        rc[r, 1, 0] = ob[ring, 1, x]

    def combine(r):
        ring = r % RING_Z
        unit = r // NCH
        wait(rc.at[r, :, pl.ds(1, 3)], e_r.at[r])

        @pl.when(r >= RING_Z)
        def _():
            sent_back(r - RING_Z)

        def one(i, carry):
            for v in range(2):
                q = (gather_at[v] + i + SIDE - 1) % SIDE
                rows = rc[r, v, :, q].reshape(LINE, CH)
                both = jnp.dot(cw[unit, v, i], rows, preferred_element_type=F32)
                part = (both[:PT] + both[PT:]).astype(BF).reshape(DEEP, ROWS, CH)
                for zz in range(DEEP):
                    zb[ring, v, zz, i] = part[zz]
            return carry

        lax.fori_loop(0, SIDE, one, 0)

    def sent_back(r):
        def early():
            wait(zb.at[0, :, 0], f_s.at[r])

        def after():
            wait(zb.at[0, :, :, 3], v_s.at[r])
            wait(zb.at[0, :, 0, pl.ds(0, 3)], f_s.at[r])

        choose(late_back(r), early, after)

    def stage_f(r):
        combine(r)
        ring = r % RING_Z

        def early():
            for v in range(2):
                send(zb.at[ring, v, 1 - z], zr.at[r, v], f_s.at[r], f_r.at[r], other)

        def after():
            for v in range(2):
                send(zb.at[ring, v, :, 3, top], xf.at[r, v, 0], v_s.at[r], v_r.at[r], gather_peer(v, 1))
                send(zb.at[ring, v, :, 3, bottom], xf.at[r, v, 1], v_s.at[r], v_r.at[r], gather_peer(v, 3))

        choose(late_back(r), early, after)

    def stage_g(r):
        ring, xring = r % RING_Z, r % RING_X

        @pl.when(r >= RING_X)
        def _():
            wait(xb.at[0, :, pl.ds(0, 2)], g_s.at[r - RING_X])
            pl.when(jnp.logical_not(late_back(r - RING_X)))(lambda: wait(xb.at[0, :, 0], v_s.at[r - RING_X]))

        def early():
            wait(zr.at[r], f_r.at[r])
            for v in range(2):
                xb[xring, v, 3] = (zb[ring, v, z, 3].astype(F32) + zr[r, v, 3].astype(F32)).astype(BF)
                send(xb.at[xring, v, 3, top], xf.at[r, v, 0, 0], v_s.at[r], v_r.at[r], gather_peer(v, 1))
                send(xb.at[xring, v, 3, bottom], xf.at[r, v, 1, 0], v_s.at[r], v_r.at[r], gather_peer(v, 3))

        def after():
            wait(xf.at[r], v_r.at[r])
            for v in range(2):
                for zz in range(DEEP):
                    zb[ring, v, zz, 2, top] = (zb[ring, v, zz, 2, top].astype(F32) + xf[r, v, 0, zz].astype(F32)).astype(BF)
                    zb[ring, v, zz, 0, bottom] = (zb[ring, v, zz, 0, bottom].astype(F32) + xf[r, v, 1, zz].astype(F32)).astype(BF)
                part = pl.ds(0, 3)
                send(zb.at[ring, v, 1 - z, part], zr.at[r, v, part], f_s.at[r], f_r.at[r], other)

        choose(late_back(r), early, after)

    def stage_v(r):
        ring, xring = r % RING_Z, r % RING_X
        choose(late_back(r), lambda: wait(xf.at[r, :, :, 0], v_r.at[r]), lambda: wait(zr.at[r, :, pl.ds(0, 3)], f_r.at[r]))
        for v in range(2):
            for i in range(3):
                xb[xring, v, i] = (zb[ring, v, z, i].astype(F32) + zr[r, v, i].astype(F32)).astype(BF)

            @pl.when(jnp.logical_not(late_back(r)))
            def _():
                for i, rows, j in ((2, top, 0), (0, bottom, 1)):
                    xb[xring, v, i, rows] = (
                        zb[ring, v, z, i, rows].astype(F32) + zr[r, v, i, rows].astype(F32) + xf[r, v, j, 0].astype(F32)
                    ).astype(BF)

            send(xb.at[xring, v, 2], xr.at[r, v, 0], g_s.at[r], g_r.at[r], gather_peer(v, 1))
            send(xb.at[xring, v, 0], xr.at[r, v, 1], g_s.at[r], g_r.at[r], gather_peer(v, 3))

    half = lambda zz: pl.ds(pl.multiple_of(zz * ROWS, ROWS), ROWS)
    at_last = lambda v: pl.ds(v * HALF + (LAST - NCH) * CH, CH)

    def last_f():
        combine(LAST)
        for v in range(2):
            for k in shifts:
                part = zb.at[LAST % RING_Z, v, :, SLOT[k]]
                send(part, xl.at[v, k - 1], f_s.at[LAST], f_r.at[LAST], gather_peer(v, k))

    def last_g():
        wait(xl, f_r.at[LAST])
        for v in range(2):
            for zz in range(DEEP):
                out = zb[LAST % RING_Z, v, zz, 1].astype(F32)
                for k in range(SIDE - 1):
                    out = out + xl[v, k, zz].astype(F32)
                acc[zz, :ROWS, :CH] = out
                wbu[0, v, zz * ROWS : (zz + 1) * ROWS, :CH] = out.astype(BF)
            send(wbu.at[0, v, half(1 - z), pl.ds(0, CH)], xr.at[LAST, v, 0], g_s.at[LAST], g_r.at[LAST], other_ahead)
            own = act[:, at_last(v)].astype(F32) + acc[z, :ROWS, :CH]
            high = own.astype(BF)
            wbu[0, v, :ROWS, CH : 2 * CH] = high
            wbu[0, v, :ROWS, 2 * CH : 3 * CH] = (own - high.astype(F32)).astype(BF)
            for part in range(2):
                for h, rows in enumerate((top, bottom)):
                    src = wbu.at[0, v, rows, pl.ds((part + 1) * CH, CH)]
                    send(src, xf.at[LAST, v, part, h], v_s.at[LAST], v_r.at[LAST], ahead)

    def last_h():
        wait(xr.at[LAST, :, 0], g_r.at[LAST])
        wait(xf.at[LAST], v_r.at[LAST])
        for v in range(2):
            own = (xf[LAST, v, 0].astype(F32) + xf[LAST, v, 1].astype(F32)).reshape(ROWS, CH)
            wbu[1, v, :ROWS, :CH] = (own + xr[LAST, v, 0].astype(F32)).astype(BF)
            pltpu.make_async_copy(wbu.at[1, v, pl.ds(0, ROWS), pl.ds(0, CH)], next_f.at[:, at_last(v)], i_s.at[v]).start()

    def summed(r, v):
        return xb[r % RING_X, v, 1].astype(F32) + xr[r, v, 0].astype(F32) + xr[r, v, 1].astype(F32)

    def stage_h_b(r):
        wait(xr.at[r], g_r.at[r])
        for v in range(2):
            gs[r, v] = summed(r, v)

    def stage_h_f(r):
        wait(xr.at[r], g_r.at[r])
        j = r - NCH
        for v in range(2):
            cols = pl.ds(pl.multiple_of(v * HALF + j * CH, CH), CH)
            act[:, cols] = (act[:, cols].astype(F32) + summed(r, v)).astype(BF)
            send(act.at[:, cols], next_f.at[:, cols], p_s.at[0], p_r.at[0], ahead)

    def finish_b():
        scaled, recip = normed(saved)
        total = jnp.zeros((ROWS, 1), F32)
        parts = []
        for v in range(2):
            for j in range(NCH):
                lo = v * HALF + j * CH
                g_n = gs[j, v] * gain[:, lo : lo + CH]
                gs[j, v] = g_n
                total = total + jnp.sum(g_n * scaled[:, lo : lo + CH], axis=-1, keepdims=True)
        mean = total * (1.0 / D)
        for v in range(2):
            for j in range(NCH):
                lo = v * HALF + j * CH
                g_x = recip * (gs[j, v] - scaled[:, lo : lo + CH] * mean)
                cot[:, lo : lo + CH] = (cot[:, lo : lo + CH].astype(F32) + g_x).astype(BF)
        send(cot, next_b, p_s.at[1], p_r.at[1], behind)

    def when(condition, stage, *args):
        pl.when(condition)(lambda: stage(*args))

    def within(i, lo, hi):
        return jnp.logical_and(i >= lo, i < hi)

    pl.semaphore_wait(barrier, len(peers))
    first_a()
    send(own_tab.at[:, 1 - z], far_tab, t_s.at[0], t_r.at[0], other)
    stage_a(1)
    fetch(0, False)
    first_b()
    wait(far_tab, t_r.at[0])
    for v in range(2):
        pair_tab[v] = own_tab[v, z] + far_tab[v]
        tab[v, 1] = pair_tab[v, gather_at[v]]
        for k in shifts:
            part = pair_tab.at[v, (gather_at[v] + k) % SIDE]
            send(part, tab.at[v, SLOT[SIDE - k]], t_s.at[1], t_r.at[1], gather_peer(v, k))

    slot_row = lax.broadcasted_iota(jnp.int32, (PAIR, 128), 0).astype(F32) + 1.0
    def trade_row(v, d, field):
        return pl.ds(((trade_at[v] + d) % SIDE) * 4 + field, 1)

    def pick_tables(batch):
        def one(i, carry):
            for v in range(2):
                for d in range(SIDE):
                    hit = tab[v, i, trade_row(v, d, batch), :] == slot_row
                    sel[batch, v, i, d * PAIR : (d + 1) * PAIR, :] = jnp.where(hit, 1.0, 0.0).astype(BF)
            return carry

        lax.fori_loop(0, SIDE, one, 0)

    def scale_tables():
        def one(i, carry):
            for v in range(2):
                for d in range(SIDE):
                    gate = tab[v, i, trade_row(v, d, 3), :]
                    picked = sel[1, v, i, d * PAIR : (d + 1) * PAIR, :].astype(F32) * gate
                    scl[v, i, d * PAIR : (d + 1) * PAIR, :] = jnp.broadcast_to(
                        jnp.sum(picked, axis=1, keepdims=True), (PAIR, 128)
                    )
            return carry

        lax.fori_loop(0, SIDE, one, 0)

    def sum_tables(i):
        rest = jnp.zeros((2 * PT - LINE, PT), F32)
        for v in range(2):
            ones, gates = [], []
            for d in range(SIDE):
                ones.append(jnp.where(tab[v, i, trade_row(v, d, 1), :] == slot_row, 1.0, 0.0))
                hit = tab[v, i, trade_row(v, d, 0), :] == slot_row
                gates.append(jnp.where(hit, tab[v, i, trade_row(v, d, 2), :], 0.0))
            gate = jnp.concatenate(gates + [rest], axis=0).T[:, :LINE]
            one = jnp.concatenate(ones + [rest], axis=0).T[:, :LINE]
            high = gate.astype(BF)
            cw[1, v, i, :PT] = high
            cw[1, v, i, PT:] = (gate - high.astype(F32)).astype(BF)
            cw[0, v, i, :PT] = one.astype(BF)
            cw[0, v, i, PT:] = jnp.zeros((PT, LINE), BF)

    def tables():
        wait(tab.at[:, pl.ds(0, 3)], t_r.at[1])
        pick_tables(1)

    def load_cot():
        loads[1].wait()
        spread(1, cot[...])

    def load_act():
        loads[2].wait()
        spread(2, normed(act)[0] * gain[...])

    def clear():
        acc[...] = jnp.zeros_like(acc)
        gh[...] = jnp.zeros_like(gh)

    def between_b():
        def one(q, carry):
            p = acc[q]
            sigma = jax.nn.sigmoid(p)
            hid[q] = (gh[q] * sigma * (1.0 + p * (1.0 - sigma))).astype(BF)
            acc[q] = jnp.zeros_like(p)
            return carry

        lax.fori_loop(0, SIDE, one, 0)

    def between_f():
        def one(q, carry):
            p = acc[q]
            hid[q] = (p * jax.nn.sigmoid(p)).astype(BF)
            return carry

        lax.fori_loop(0, SIDE, one, 0)

    def step(s, carry):
        when(within(s - AT_B, 1, NOUT), stage_b, s - AT_B)
        when(within(s - AT_F, 0, LAST), stage_f, s - AT_F)
        when(s - AT_F == LAST, last_f)
        when(within(s - AT_W, 1, NOUT), stage_w, s - AT_W)
        when(s - AT_A == NCH, load_cot)
        when(s - AT_A == 2 * NCH, load_act)
        when(within(s - AT_A, 2, NOUT), stage_a, s - AT_A)
        when(within(s - AT_V, 0, LAST), stage_v, s - AT_V)
        when(within(s - AT_G, 0, LAST), stage_g, s - AT_G)
        when(s - AT_G == LAST, last_g)

        when(s == AT_C, tables)
        n = s - AT_C
        when(within(n, 0, NCH), stage_c, n, 0)
        when(within(n, NCH, 2 * NCH), stage_c, n, 1)
        when(within(n, 2 * NCH, NOUT), stage_c, n, 2)

        i = s - AT_D
        for down in (False, True):
            kind = (i // NCH) % 2 == (1 if down else 0)
            kind_next = ((i + 1) // NCH) % 2 == (1 if down else 0)
            when(jnp.logical_and(within(i, 0, 4 * NCH - 1), kind_next), fetch, i + 1, down)
            now = jnp.logical_and(within(i, 0, 4 * NCH), kind)
            when(now, lambda down=down: wait((wbd if down else wbu).at[i % 2], w_sem.at[i % 2]))
        when(i == 2 * NCH, between_b)
        when(i == 3 * NCH, between_f)
        when(within(i, 2 * NCH, 3 * NCH), stage_e, i - 2 * NCH, False)
        when(within(i, 3 * NCH, 4 * NCH), stage_e, i - 2 * NCH, True)
        when(within(i, 0, NCH), stage_d, i, False, acc)
        when(within(i, NCH, 2 * NCH), stage_d, i, True, gh)
        when(within(i, 2 * NCH, NOUT), stage_d, i, False, acc)

        r = s - AT_H
        when(within(r, 0, NCH), stage_h_b, r)
        when(within(r, NCH, LAST), stage_h_f, r)
        when(r == LAST, last_h)
        when(r == NCH, finish_b)

        when(s == AT_C - 1, clear)
        when(s == AT_C + 2, scale_tables)
        when(s == AT_C + 4, pick_tables, 0)
        when(within(s - (AT_C + 5), 0, SIDE), sum_tables, s - (AT_C + 5))
        return carry

    lax.fori_loop(0, AT_H + NRET, step, 0)

    def sent(n, carry):
        wait(ag.at[0, 0, pl.ds(0, 2)], a_s.at[n])
        wait(ag.at[0, :, pl.ds(0, 3), 0], b_s.at[n])

        def early():
            wait(ag.at[0, :, 3, 0], h_s.at[n])
            wait(ag.at[0, :, 3, 0], k_s.at[n])

        choose(late_out(n), early, lambda: wait(ag.at[0, :, 3], h_s.at[n]))
        return carry

    lax.fori_loop(1, NOUT, sent, 0)
    wait(ag.at[0, 0, 0], a_s.at[0])
    wait(ag.at[0, :, pl.ds(0, 3)], b_s.at[0])
    wait(far_tab, t_s.at[0])
    wait(tab.at[:, pl.ds(0, 3)], t_s.at[1])
    for n in range(NOUT - RING_S, NOUT):
        wait(snd.at[0], c_s.at[n])
    for r in range(NRET - RING_O, NRET):
        wait(ob.at[0, :, pl.ds(0, 3)], e_s.at[r])
    for r in range(NRET - RING_Z, LAST):
        if r in LATE_BACK:
            wait(zb.at[0, :, :, 3], v_s.at[r])
            wait(zb.at[0, :, 0, pl.ds(0, 3)], f_s.at[r])
        else:
            wait(zb.at[0, :, 0], f_s.at[r])
    wait(xl, f_s.at[LAST])
    for r in range(LAST - RING_X, LAST):
        wait(xb.at[0, :, pl.ds(0, 2)], g_s.at[r])
        if r not in LATE_BACK:
            wait(xb.at[0, :, 0], v_s.at[r])
    wait(xr.at[0, :, 0], g_s.at[LAST])
    wait(xf.at[LAST], v_s.at[LAST])
    most = pl.ds(0, D - 2 * CH)
    wait(cot.at[:, most], p_s.at[0])
    wait(cot, p_s.at[1])
    wait(next_f.at[:, most], p_r.at[0])
    wait(next_b, p_r.at[1])
    for v in range(2):
        wait(next_f.at[:, at_last(v)], i_s.at[v])


def per_device(
    act_fwd, routes_fwd, mix_fwd, cot_bwd, saved_bwd, routes_bwd, mix_bwd, norm_gain, w_up, w_down
):
    vmem, far = pl.BlockSpec(memory_space=pltpu.VMEM), pl.BlockSpec(memory_space=pl.ANY)
    sems = [pltpu.SemaphoreType.DMA((NOUT,))] * 6 + [pltpu.SemaphoreType.DMA((NRET,))] * 6
    sems += [pltpu.SemaphoreType.DMA((NOUT,))] * 4 + [pltpu.SemaphoreType.DMA((NRET,))] * 2
    sems += [pltpu.SemaphoreType.DMA((2,))] * 5
    out = jax.ShapeDtypeStruct((2, ROWS, D), BF)
    both = pl.pallas_call(
        kernel,
        out_shape=out,
        in_specs=[far, vmem, vmem, far, far, vmem, vmem, vmem, far, far],
        out_specs=far,
        scratch_shapes=[
            pltpu.VMEM((ROWS, D), BF),
            pltpu.VMEM((ROWS, D), BF),
            pltpu.VMEM((ROWS, D), BF),
            pltpu.SemaphoreType.DMA((3,)),
            pltpu.VMEM((2, SIDE - 1, DEEP, ROWS, CH), BF),
            pltpu.VMEM((NOUT, 2, SIDE, DEEP, ROWS, CH), BF),
            pltpu.VMEM((NOUT, 2, SIDE, SIDE, PAIR, CH), BF),
            pltpu.VMEM((RING_S, 2, SIDE - 1, SIDE, PAIR, CH), BF),
            pltpu.VMEM((2, 2, CH, HID), BF),
            pltpu.VMEM((2, 2, HID, CH), BF),
            pltpu.VMEM((RING_O, 2, SIDE, SIDE, PAIR, CH), BF),
            pltpu.VMEM((RING_Z, 2, DEEP, SIDE, ROWS, CH), BF),
            pltpu.VMEM((NRET, 2, SIDE, ROWS, CH), BF),
            pltpu.VMEM((RING_X, 2, SIDE, ROWS, CH), BF),
            pltpu.VMEM((NRET, 2, 2, ROWS, CH), BF),
            pltpu.VMEM((NCH, 2, ROWS, CH), F32),
            pltpu.VMEM((SIDE, LINE, HID), F32),
            pltpu.VMEM((SIDE, LINE, HID), F32),
            pltpu.VMEM((SIDE, LINE, HID), BF),
            pltpu.VMEM((2, 2, SIDE, LINE, PT), BF),
            pltpu.VMEM((2, SIDE, LINE, 128), F32),
            pltpu.VMEM((2, 2, SIDE, 2 * PT, LINE), BF),
            pltpu.VMEM((2, SIDE, 16, PT), F32),
            pltpu.VMEM((2, DEEP, SIDE, 16, PT), F32),
            pltpu.VMEM((2, SIDE, 16, PT), F32),
            pltpu.VMEM((2, SIDE, 16, PT), F32),
            pltpu.VMEM((NRET, 2, 2, DEEP, ROWS // 2, CH), BF),
        ]
        + sems,
        compiler_params=pltpu.CompilerParams(
            collective_id=0, has_side_effects=True, vmem_limit_bytes=63 * 2**20
        ),
        cost_estimate=pl.CostEstimate(flops=30 * 10**9, bytes_accessed=40 * 10**6, transcendentals=2 * 10**6),
    )(
        act_fwd[0], routes_fwd[0].T, mix_fwd[0].T, cot_bwd[0], saved_bwd[0], routes_bwd[0].T, mix_bwd[0].T,
        norm_gain, w_up[0, 0], w_down[0, 0],
    )
    return both[0:1], both[1:2]


def solution(mesh):
    rows = P("pipe", "expert", None)
    return jax.shard_map(
        per_device,
        mesh=mesh,
        in_specs=(rows,) * 7 + (P("pipe", None),) + (P("pipe", "expert", None, None),) * 2,
        out_specs=(rows, rows),
        check_vma=False,
    )
```

```python
import functools

import jax
import jax.numpy as jnp
from jax import lax
from jax.experimental import pallas as pl
from jax.experimental.pallas import tpu as pltpu
from jax.sharding import PartitionSpec as P

MESH = pl.DeviceIdType.MESH
BF, F32 = jnp.bfloat16, jnp.float32

D, HID, TOP, ROWS, CAP = 3584, 1024, 8, 64, 24
SIDE, DEEP = 4, 2
HALF = D // 2
CH = 256
NCH = HALF // CH
PAIR = DEEP * CAP
LINE = SIDE * PAIR
PT = DEEP * ROWS
NOUT, NRET = 3 * NCH, 2 * NCH
RING_S, RING_O, RING_Z, RING_X = 3, 4, 7, 5
LAST = NRET - 1
AT_A, AT_B, AT_W, AT_C, AT_D = 0, 6, 7, 8, 11
AT_E = AT_D + 2 * NCH
AT_F, AT_G, AT_V, AT_H = AT_E + 4, AT_E + 7, AT_E + 10, AT_E + 13
SLOT = {0: 1, 1: 2, 2: 3, 3: 0}


LATE_OUT, LATE_BACK = (1, 2, 10, 11, 12, 13, 15, 16), (5, 8, 11)


def among(n, chunks):
    found = n == chunks[0]
    for one in chunks[1:]:
        found = jnp.logical_or(found, n == one)
    return found


def kernel(
    act_far, routes_f_far, mix_f_far, cot_far, saved_far, routes_b_far, mix_b_far, gain_far, wup, wdn,
    both_next,
    act, cot, saved, routes_f, mix_f, routes_b, mix_b, gain, i_s, xl,
    ag, rc, snd, wbu, wbd, ob, zb, zr, xb, xr, gs, acc, gh, hid, sel, scl, cw, tab, own_tab, far_tab, pair_tab, xf,
    a_s, a_r, b_s, b_r, c_s, c_r, e_s, e_r, f_s, f_r, g_s, g_r, h_s, h_r, k_s, k_r, v_s, v_r, w_sem, t_s, t_r, p_s, p_r,
):
    next_f, next_b = both_next.at[0], both_next.at[1]
    pp, me = lax.axis_index("pipe"), lax.axis_index("expert")
    z, x, y = me // (SIDE * SIDE), (me // SIDE) % SIDE, me % SIDE
    n_pipe = lax.axis_size("pipe")

    def device(dz, dx, dy):
        return (pp, ((z + dz) % DEEP) * SIDE * SIDE + ((x + dx) % SIDE) * SIDE + (y + dy) % SIDE)

    gather_at, trade_at = (x, y), (y, x)
    gather_peer = lambda v, k: device(0, k, 0) if v == 0 else device(0, 0, k)
    trade_peer = lambda v, k: device(0, 0, k) if v == 0 else device(0, k, 0)
    other = device(1, 0, 0)
    ahead, behind = ((pp + 1) % n_pipe, me), ((pp + n_pipe - 1) % n_pipe, me)
    shifts = range(1, SIDE)

    def send(src, dst, s_sem, r_sem, to):
        pltpu.make_async_remote_copy(
            src_ref=src, dst_ref=dst, send_sem=s_sem, recv_sem=r_sem, device_id=to, device_id_type=MESH
        ).start()

    def wait(ref, sem):
        pltpu.make_async_copy(ref, ref, sem).wait()

    barrier = pltpu.get_barrier_semaphore()
    other_ahead, other_behind = (ahead[0], other[1]), (behind[0], other[1])
    peers = [other, ahead, behind, other_behind] + [gather_peer(v, k) for v in range(2) for k in shifts]
    for peer in peers:
        pl.semaphore_signal(barrier, inc=1, device_id=peer, device_id_type=MESH)

    pairs = (saved_far, saved), (cot_far, cot), (act_far, act), (gain_far, gain)
    pairs += (routes_f_far, routes_f), (mix_f_far, mix_f), (routes_b_far, routes_b), (mix_b_far, mix_b)
    loads = [pltpu.make_async_copy(far, near, i_s.at[i]) for i, (far, near) in enumerate(pairs)]
    for load in loads[3:] + loads[:3]:
        load.start()
    for load in loads[3:]:
        load.wait()

    line = lax.broadcasted_iota(jnp.int32, (128, PT), 0)
    mine = lax.broadcasted_iota(jnp.int32, (128, PT), 1) // ROWS == z
    major, minor, field = (line // 16) % SIDE, (line // 4) % SIDE, line % 4
    is_b = field % 2 == 1
    earlier = lax.broadcasted_iota(jnp.int32, (PT, PT), 0) < lax.broadcasted_iota(jnp.int32, (PT, PT), 1)
    earlier = jnp.where(earlier, 1.0, 0.0).astype(BF)
    twice = lambda ref, k: jnp.concatenate([ref[k : k + 1, :]] * DEEP, axis=1)
    for v in range(2):
        expert_of = (line // 64) * SIDE * SIDE + (major * SIDE + minor if v == 0 else minor * SIDE + major)
        chosen = jnp.zeros((128, PT), F32)
        weight = jnp.zeros((128, PT), F32)
        for k in range(TOP):
            hit = jnp.logical_and(jnp.where(is_b, twice(routes_b, k), twice(routes_f, k)) == expert_of, mine)
            chosen = jnp.where(hit, 1.0, chosen)
            weight = jnp.where(hit, jnp.where(is_b, twice(mix_b, k), twice(mix_f, k)), weight)
        rank = jnp.dot(chosen.astype(BF), earlier, preferred_element_type=F32)
        slot = jnp.where(chosen > 0.5, rank + (z * CAP + 1).astype(F32), 0.0)
        table = jnp.where(field < 2, slot, weight)
        for zz in range(DEEP):
            own_tab[v, zz] = table[zz * 64 : (zz + 1) * 64].reshape(SIDE, 16, PT)

    def spread(array, wide):
        for v in range(2):
            for j in range(NCH):
                lo = v * HALF + j * CH
                ag[array * NCH + j, v, 1, z] = wide[:, lo : lo + CH].astype(BF)

    def normed(ref):
        wide = ref[...].astype(F32)
        recip = lax.rsqrt(jnp.sum(wide * wide, axis=-1, keepdims=True) * (1.0 / D) + 1e-06)
        return wide * recip, recip

    loads[0].wait()
    spread(0, normed(saved)[0] * gain[...])

    def choose(late, early, after):
        pl.when(late)(after)
        pl.when(jnp.logical_not(late))(early)

    late_out, late_back = (lambda n: among(n, LATE_OUT)), (lambda r: among(r, LATE_BACK))

    top, bottom = pl.ds(0, ROWS // 2), pl.ds(ROWS // 2, ROWS // 2)

    def stage_a(n):
        for v in range(2):
            own = ag.at[n, v, 1, z]
            send(own, ag.at[n, v, 0, z], a_s.at[n], a_r.at[n], gather_peer(v, 1))
            send(own, ag.at[n, v, 2, z], a_s.at[n], a_r.at[n], gather_peer(v, 3))

    def stage_b(n):
        wait(ag.at[n, 0, pl.ds(0, 2)], a_r.at[n])
        for v in range(2):
            part = ag.at[n, v, pl.ds(0, 3), z]
            send(part, part, b_s.at[n], b_r.at[n], other)

        @pl.when(jnp.logical_not(late_out(n)))
        def _():
            for v in range(2):
                send(ag.at[n, v, 0, z, top], ag.at[n, v, 3, z, top], h_s.at[n], h_r.at[n], gather_peer(v, 1))
                send(ag.at[n, v, 2, z, bottom], ag.at[n, v, 3, z, bottom], h_s.at[n], h_r.at[n], gather_peer(v, 3))

    def stage_w(n):
        def early():
            wait(ag.at[n, :, 3, 0], h_r.at[n])
            for v in range(2):
                send(ag.at[n, v, 3, z], ag.at[n, v, 3, z], k_s.at[n], k_r.at[n], other)

        def after():
            wait(ag.at[n, :, pl.ds(0, 3), 0], b_r.at[n])
            for v in range(2):
                send(ag.at[n, v, 0, :, top], ag.at[n, v, 3, :, top], h_s.at[n], h_r.at[n], gather_peer(v, 1))
                send(ag.at[n, v, 2, :, bottom], ag.at[n, v, 3, :, bottom], h_s.at[n], h_r.at[n], gather_peer(v, 3))

        choose(late_out(n), early, after)

    def gathered(n):
        def early():
            wait(ag.at[n, :, pl.ds(0, 3), 0], b_r.at[n])
            wait(ag.at[n, :, 3, 0], k_r.at[n])

        choose(late_out(n), early, lambda: wait(ag.at[n, :, 3], h_r.at[n]))

    def first_a():
        for v in range(2):
            own = ag.at[0, v, 1, z]
            send(own, own, a_s.at[0], a_r.at[0], other)

    def first_b():
        wait(ag.at[0, 0, 0], a_r.at[0])
        for v in range(2):
            for k in shifts:
                send(ag.at[0, v, 1], ag.at[0, v, SLOT[SIDE - k]], b_s.at[0], b_r.at[0], gather_peer(v, k))

    def stage_c(n, array):
        batch = 1 if array < 2 else 0
        ring = n % RING_S
        if array == 0:
            pl.when(n == 0)(lambda: wait(ag.at[0, :, pl.ds(0, 3)], b_r.at[0]))
            pl.when(n > 0)(lambda: gathered(n))
        else:
            gathered(n)

        @pl.when(n >= RING_S)
        def _():
            wait(snd.at[ring], c_s.at[n - RING_S])

        def one(i, carry):
            for v in range(2):
                q = (gather_at[v] + i + SIDE - 1) % SIDE
                rows = ag[n, v, i].reshape(PT, CH)
                got = jnp.dot(sel[batch, v, i], rows, preferred_element_type=F32)
                if array == 1:
                    got = got * scl[v, i][:, 0:1]
                got = got.astype(BF).reshape(SIDE, PAIR, CH)
                if v == 0:
                    rc[n, 0, q, y] = got[0]
                else:
                    rc[n, 1, x, q] = got[0]
                for d in shifts:
                    snd[ring, v, d - 1, q] = got[d]
            return carry

        lax.fori_loop(0, SIDE, one, 0)
        for k in shifts:
            send(snd.at[ring, 0, k - 1], rc.at[n, 0, :, y], c_s.at[n], c_r.at[n], trade_peer(0, k))
            send(snd.at[ring, 1, k - 1], rc.at[n, 1, x], c_s.at[n], c_r.at[n], trade_peer(1, k))

    def fetch(i, down):
        j, ring = i % NCH, i % 2
        for v in range(2):
            cols = pl.ds(pl.multiple_of(v * HALF + j * CH, CH), CH)
            if down:
                pltpu.make_async_copy(wdn.at[:, cols], wbd.at[ring, v], w_sem.at[ring]).start()
            else:
                pltpu.make_async_copy(wup.at[cols, :], wbu.at[ring, v], w_sem.at[ring]).start()

    NT = (((1,), (1,)), ((), ()))

    def stage_d(n, down, total):
        ring = n % 2
        six = rc.at[n, :, pl.ds(0, 3)]
        wait(six, c_r.at[n])

        def one(q, carry):
            out = total[q]
            for v in range(2):
                rows = rc[n, v, q].reshape(LINE, CH)
                if down:
                    out = out + lax.dot_general(rows, wbd[ring, v], NT, preferred_element_type=F32)
                else:
                    out = out + jnp.dot(rows, wbu[ring, v], preferred_element_type=F32)
            total[q] = out
            return carry

        lax.fori_loop(0, SIDE, one, 0)

    def stage_e(r, down):
        ring, wring = r % RING_O, r % 2

        @pl.when(r >= RING_O)
        def _():
            wait(ob.at[ring, :, pl.ds(0, 3)], e_s.at[r - RING_O])

        def one(q, carry):
            for v in range(2):
                if down:
                    got = jnp.dot(hid[q], wbd[wring, v], preferred_element_type=F32)
                else:
                    got = lax.dot_general(hid[q], wbu[wring, v], NT, preferred_element_type=F32)
                ob[ring, v, q] = got.astype(BF).reshape(SIDE, PAIR, CH)
            return carry

        lax.fori_loop(0, SIDE, one, 0)
        for k in shifts:
            send(ob.at[ring, 0, :, (y + k) % SIDE], rc.at[r, 0, SIDE - k], e_s.at[r], e_r.at[r], trade_peer(0, k))
            send(ob.at[ring, 1, (x + k) % SIDE], rc.at[r, 1, SIDE - k], e_s.at[r], e_r.at[r], trade_peer(1, k))
        for q in range(SIDE):
            rc[r, 0, 0, q] = ob[ring, 0, q, y]
        rc[r, 1, 0] = ob[ring, 1, x]

    def combine(r):
        ring = r % RING_Z
        unit = r // NCH
        wait(rc.at[r, :, pl.ds(1, 3)], e_r.at[r])

        @pl.when(r >= RING_Z)
        def _():
            sent_back(r - RING_Z)

        def one(i, carry):
            for v in range(2):
                q = (gather_at[v] + i + SIDE - 1) % SIDE
                rows = rc[r, v, :, q].reshape(LINE, CH)
                both = jnp.dot(cw[unit, v, i], rows, preferred_element_type=F32)
                part = (both[:PT] + both[PT:]).astype(BF).reshape(DEEP, ROWS, CH)
                for zz in range(DEEP):
                    zb[ring, v, zz, i] = part[zz]
            return carry

        lax.fori_loop(0, SIDE, one, 0)

    def sent_back(r):
        def early():
            wait(zb.at[0, :, 0], f_s.at[r])

        def after():
            wait(zb.at[0, :, :, 3], v_s.at[r])
            wait(zb.at[0, :, 0, pl.ds(0, 3)], f_s.at[r])

        choose(late_back(r), early, after)

    def stage_f(r):
        combine(r)
        ring = r % RING_Z

        def early():
            for v in range(2):
                send(zb.at[ring, v, 1 - z], zr.at[r, v], f_s.at[r], f_r.at[r], other)

        def after():
            for v in range(2):
                send(zb.at[ring, v, :, 3, top], xf.at[r, v, 0], v_s.at[r], v_r.at[r], gather_peer(v, 1))
                send(zb.at[ring, v, :, 3, bottom], xf.at[r, v, 1], v_s.at[r], v_r.at[r], gather_peer(v, 3))

        choose(late_back(r), early, after)

    def stage_g(r):
        ring, xring = r % RING_Z, r % RING_X

        @pl.when(r >= RING_X)
        def _():
            wait(xb.at[0, :, pl.ds(0, 2)], g_s.at[r - RING_X])
            pl.when(jnp.logical_not(late_back(r - RING_X)))(lambda: wait(xb.at[0, :, 0], v_s.at[r - RING_X]))

        def early():
            wait(zr.at[r], f_r.at[r])
            for v in range(2):
                xb[xring, v, 3] = (zb[ring, v, z, 3].astype(F32) + zr[r, v, 3].astype(F32)).astype(BF)
                send(xb.at[xring, v, 3, top], xf.at[r, v, 0, 0], v_s.at[r], v_r.at[r], gather_peer(v, 1))
                send(xb.at[xring, v, 3, bottom], xf.at[r, v, 1, 0], v_s.at[r], v_r.at[r], gather_peer(v, 3))

        def after():
            wait(xf.at[r], v_r.at[r])
            for v in range(2):
                for zz in range(DEEP):
                    zb[ring, v, zz, 2, top] = (zb[ring, v, zz, 2, top].astype(F32) + xf[r, v, 0, zz].astype(F32)).astype(BF)
                    zb[ring, v, zz, 0, bottom] = (zb[ring, v, zz, 0, bottom].astype(F32) + xf[r, v, 1, zz].astype(F32)).astype(BF)
                part = pl.ds(0, 3)
                send(zb.at[ring, v, 1 - z, part], zr.at[r, v, part], f_s.at[r], f_r.at[r], other)

        choose(late_back(r), early, after)

    def stage_v(r):
        ring, xring = r % RING_Z, r % RING_X
        choose(late_back(r), lambda: wait(xf.at[r, :, :, 0], v_r.at[r]), lambda: wait(zr.at[r, :, pl.ds(0, 3)], f_r.at[r]))
        for v in range(2):
            for i in range(3):
                xb[xring, v, i] = (zb[ring, v, z, i].astype(F32) + zr[r, v, i].astype(F32)).astype(BF)

            @pl.when(jnp.logical_not(late_back(r)))
            def _():
                for i, rows, j in ((2, top, 0), (0, bottom, 1)):
                    xb[xring, v, i, rows] = (
                        zb[ring, v, z, i, rows].astype(F32) + zr[r, v, i, rows].astype(F32) + xf[r, v, j, 0].astype(F32)
                    ).astype(BF)

            send(xb.at[xring, v, 2], xr.at[r, v, 0], g_s.at[r], g_r.at[r], gather_peer(v, 1))
            send(xb.at[xring, v, 0], xr.at[r, v, 1], g_s.at[r], g_r.at[r], gather_peer(v, 3))

    half = lambda zz: pl.ds(pl.multiple_of(zz * ROWS, ROWS), ROWS)
    at_last = lambda v: pl.ds(v * HALF + (LAST - NCH) * CH, CH)

    def last_f():
        combine(LAST)
        for v in range(2):
            for k in shifts:
                part = zb.at[LAST % RING_Z, v, :, SLOT[k]]
                send(part, xl.at[v, k - 1], f_s.at[LAST], f_r.at[LAST], gather_peer(v, k))

    def last_g():
        wait(xl, f_r.at[LAST])
        for v in range(2):
            for zz in range(DEEP):
                out = zb[LAST % RING_Z, v, zz, 1].astype(F32)
                for k in range(SIDE - 1):
                    out = out + xl[v, k, zz].astype(F32)
                acc[zz, :ROWS, :CH] = out
                wbu[0, v, zz * ROWS : (zz + 1) * ROWS, :CH] = out.astype(BF)
            send(wbu.at[0, v, half(1 - z), pl.ds(0, CH)], xr.at[LAST, v, 0], g_s.at[LAST], g_r.at[LAST], other_ahead)
            own = act[:, at_last(v)].astype(F32) + acc[z, :ROWS, :CH]
            high = own.astype(BF)
            wbu[0, v, :ROWS, CH : 2 * CH] = high
            wbu[0, v, :ROWS, 2 * CH : 3 * CH] = (own - high.astype(F32)).astype(BF)
            for part in range(2):
                for h, rows in enumerate((top, bottom)):
                    src = wbu.at[0, v, rows, pl.ds((part + 1) * CH, CH)]
                    send(src, xf.at[LAST, v, part, h], v_s.at[LAST], v_r.at[LAST], ahead)

    def last_h():
        wait(xr.at[LAST, :, 0], g_r.at[LAST])
        wait(xf.at[LAST], v_r.at[LAST])
        for v in range(2):
            own = (xf[LAST, v, 0].astype(F32) + xf[LAST, v, 1].astype(F32)).reshape(ROWS, CH)
            wbu[1, v, :ROWS, :CH] = (own + xr[LAST, v, 0].astype(F32)).astype(BF)
            pltpu.make_async_copy(wbu.at[1, v, pl.ds(0, ROWS), pl.ds(0, CH)], next_f.at[:, at_last(v)], i_s.at[v]).start()

    def summed(r, v):
        return xb[r % RING_X, v, 1].astype(F32) + xr[r, v, 0].astype(F32) + xr[r, v, 1].astype(F32)

    def stage_h_b(r):
        wait(xr.at[r], g_r.at[r])
        for v in range(2):
            gs[r, v] = summed(r, v)

    def stage_h_f(r):
        wait(xr.at[r], g_r.at[r])
        j = r - NCH
        for v in range(2):
            cols = pl.ds(pl.multiple_of(v * HALF + j * CH, CH), CH)
            act[:, cols] = (act[:, cols].astype(F32) + summed(r, v)).astype(BF)
            send(act.at[:, cols], next_f.at[:, cols], p_s.at[0], p_r.at[0], ahead)

    def finish_b():
        scaled, recip = normed(saved)
        total = jnp.zeros((ROWS, 1), F32)
        parts = []
        for v in range(2):
            for j in range(NCH):
                lo = v * HALF + j * CH
                g_n = gs[j, v] * gain[:, lo : lo + CH]
                gs[j, v] = g_n
                total = total + jnp.sum(g_n * scaled[:, lo : lo + CH], axis=-1, keepdims=True)
        mean = total * (1.0 / D)
        for v in range(2):
            for j in range(NCH):
                lo = v * HALF + j * CH
                g_x = recip * (gs[j, v] - scaled[:, lo : lo + CH] * mean)
                cot[:, lo : lo + CH] = (cot[:, lo : lo + CH].astype(F32) + g_x).astype(BF)
        send(cot, next_b, p_s.at[1], p_r.at[1], behind)

    def when(condition, stage, *args):
        pl.when(condition)(lambda: stage(*args))

    def within(i, lo, hi):
        return jnp.logical_and(i >= lo, i < hi)

    pl.semaphore_wait(barrier, len(peers))
    first_a()
    send(own_tab.at[:, 1 - z], far_tab, t_s.at[0], t_r.at[0], other)
    stage_a(1)
    fetch(0, False)
    first_b()
    wait(far_tab, t_r.at[0])
    for v in range(2):
        pair_tab[v] = own_tab[v, z] + far_tab[v]
        tab[v, 1] = pair_tab[v, gather_at[v]]
        for k in shifts:
            part = pair_tab.at[v, (gather_at[v] + k) % SIDE]
            send(part, tab.at[v, SLOT[SIDE - k]], t_s.at[1], t_r.at[1], gather_peer(v, k))

    slot_row = lax.broadcasted_iota(jnp.int32, (PAIR, 128), 0).astype(F32) + 1.0
    def trade_row(v, d, field):
        return pl.ds(((trade_at[v] + d) % SIDE) * 4 + field, 1)

    def pick_tables(batch):
        def one(i, carry):
            for v in range(2):
                for d in range(SIDE):
                    hit = tab[v, i, trade_row(v, d, batch), :] == slot_row
                    sel[batch, v, i, d * PAIR : (d + 1) * PAIR, :] = jnp.where(hit, 1.0, 0.0).astype(BF)
            return carry

        lax.fori_loop(0, SIDE, one, 0)

    def scale_tables():
        def one(i, carry):
            for v in range(2):
                for d in range(SIDE):
                    gate = tab[v, i, trade_row(v, d, 3), :]
                    picked = sel[1, v, i, d * PAIR : (d + 1) * PAIR, :].astype(F32) * gate
                    scl[v, i, d * PAIR : (d + 1) * PAIR, :] = jnp.broadcast_to(
                        jnp.sum(picked, axis=1, keepdims=True), (PAIR, 128)
                    )
            return carry

        lax.fori_loop(0, SIDE, one, 0)

    def sum_tables(i):
        rest = jnp.zeros((2 * PT - LINE, PT), F32)
        for v in range(2):
            ones, gates = [], []
            for d in range(SIDE):
                ones.append(jnp.where(tab[v, i, trade_row(v, d, 1), :] == slot_row, 1.0, 0.0))
                hit = tab[v, i, trade_row(v, d, 0), :] == slot_row
                gates.append(jnp.where(hit, tab[v, i, trade_row(v, d, 2), :], 0.0))
            gate = jnp.concatenate(gates + [rest], axis=0).T[:, :LINE]
            one = jnp.concatenate(ones + [rest], axis=0).T[:, :LINE]
            high = gate.astype(BF)
            cw[1, v, i, :PT] = high
            cw[1, v, i, PT:] = (gate - high.astype(F32)).astype(BF)
            cw[0, v, i, :PT] = one.astype(BF)
            cw[0, v, i, PT:] = jnp.zeros((PT, LINE), BF)

    def tables():
        wait(tab.at[:, pl.ds(0, 3)], t_r.at[1])
        pick_tables(1)

    def load_cot():
        loads[1].wait()
        spread(1, cot[...])

    def load_act():
        loads[2].wait()
        spread(2, normed(act)[0] * gain[...])

    def clear():
        acc[...] = jnp.zeros_like(acc)
        gh[...] = jnp.zeros_like(gh)

    def between_b():
        def one(q, carry):
            p = acc[q]
            sigma = jax.nn.sigmoid(p)
            hid[q] = (gh[q] * sigma * (1.0 + p * (1.0 - sigma))).astype(BF)
            acc[q] = jnp.zeros_like(p)
            return carry

        lax.fori_loop(0, SIDE, one, 0)

    def between_f():
        def one(q, carry):
            p = acc[q]
            hid[q] = (p * jax.nn.sigmoid(p)).astype(BF)
            return carry

        lax.fori_loop(0, SIDE, one, 0)

    def step(s, carry):
        when(within(s - AT_B, 1, NOUT), stage_b, s - AT_B)
        when(within(s - AT_F, 0, LAST), stage_f, s - AT_F)
        when(s - AT_F == LAST, last_f)
        when(within(s - AT_W, 1, NOUT), stage_w, s - AT_W)
        when(s - AT_A == NCH, load_cot)
        when(s - AT_A == 2 * NCH, load_act)
        when(within(s - AT_A, 2, NOUT), stage_a, s - AT_A)
        when(within(s - AT_V, 0, LAST), stage_v, s - AT_V)
        when(within(s - AT_G, 0, LAST), stage_g, s - AT_G)
        when(s - AT_G == LAST, last_g)

        when(s == AT_C, tables)
        n = s - AT_C
        when(within(n, 0, NCH), stage_c, n, 0)
        when(within(n, NCH, 2 * NCH), stage_c, n, 1)
        when(within(n, 2 * NCH, NOUT), stage_c, n, 2)

        i = s - AT_D
        for down in (False, True):
            kind = (i // NCH) % 2 == (1 if down else 0)
            kind_next = ((i + 1) // NCH) % 2 == (1 if down else 0)
            when(jnp.logical_and(within(i, 0, 4 * NCH - 1), kind_next), fetch, i + 1, down)
            now = jnp.logical_and(within(i, 0, 4 * NCH), kind)
            when(now, lambda down=down: wait((wbd if down else wbu).at[i % 2], w_sem.at[i % 2]))
        when(i == 2 * NCH, between_b)
        when(i == 3 * NCH, between_f)
        when(within(i, 2 * NCH, 3 * NCH), stage_e, i - 2 * NCH, False)
        when(within(i, 3 * NCH, 4 * NCH), stage_e, i - 2 * NCH, True)
        when(within(i, 0, NCH), stage_d, i, False, acc)
        when(within(i, NCH, 2 * NCH), stage_d, i, True, gh)
        when(within(i, 2 * NCH, NOUT), stage_d, i, False, acc)

        r = s - AT_H
        when(within(r, 0, NCH), stage_h_b, r)
        when(within(r, NCH, LAST), stage_h_f, r)
        when(r == LAST, last_h)
        when(r == NCH, finish_b)

        when(s == AT_C - 1, clear)
        when(s == AT_C + 2, scale_tables)
        when(s == AT_C + 4, pick_tables, 0)
        when(within(s - (AT_C + 5), 0, SIDE), sum_tables, s - (AT_C + 5))
        return carry

    lax.fori_loop(0, AT_H + NRET, step, 0)

    def sent(n, carry):
        wait(ag.at[0, 0, pl.ds(0, 2)], a_s.at[n])
        wait(ag.at[0, :, pl.ds(0, 3), 0], b_s.at[n])

        def early():
            wait(ag.at[0, :, 3, 0], h_s.at[n])
            wait(ag.at[0, :, 3, 0], k_s.at[n])

        choose(late_out(n), early, lambda: wait(ag.at[0, :, 3], h_s.at[n]))
        return carry

    lax.fori_loop(1, NOUT, sent, 0)
    wait(ag.at[0, 0, 0], a_s.at[0])
    wait(ag.at[0, :, pl.ds(0, 3)], b_s.at[0])
    wait(far_tab, t_s.at[0])
    wait(tab.at[:, pl.ds(0, 3)], t_s.at[1])
    for n in range(NOUT - RING_S, NOUT):
        wait(snd.at[0], c_s.at[n])
    for r in range(NRET - RING_O, NRET):
        wait(ob.at[0, :, pl.ds(0, 3)], e_s.at[r])
    for r in range(NRET - RING_Z, LAST):
        if r in LATE_BACK:
            wait(zb.at[0, :, :, 3], v_s.at[r])
            wait(zb.at[0, :, 0, pl.ds(0, 3)], f_s.at[r])
        else:
            wait(zb.at[0, :, 0], f_s.at[r])
    wait(xl, f_s.at[LAST])
    for r in range(LAST - RING_X, LAST):
        wait(xb.at[0, :, pl.ds(0, 2)], g_s.at[r])
        if r not in LATE_BACK:
            wait(xb.at[0, :, 0], v_s.at[r])
    wait(xr.at[0, :, 0], g_s.at[LAST])
    wait(xf.at[LAST], v_s.at[LAST])
    most = pl.ds(0, D - 2 * CH)
    wait(cot.at[:, most], p_s.at[0])
    wait(cot, p_s.at[1])
    wait(next_f.at[:, most], p_r.at[0])
    wait(next_b, p_r.at[1])
    for v in range(2):
        wait(next_f.at[:, at_last(v)], i_s.at[v])


def per_device(
    act_fwd, routes_fwd, mix_fwd, cot_bwd, saved_bwd, routes_bwd, mix_bwd, norm_gain, w_up, w_down
):
    far = pl.BlockSpec(memory_space=pl.ANY)
    sems = [pltpu.SemaphoreType.DMA((NOUT,))] * 6 + [pltpu.SemaphoreType.DMA((NRET,))] * 6
    sems += [pltpu.SemaphoreType.DMA((NOUT,))] * 4 + [pltpu.SemaphoreType.DMA((NRET,))] * 2
    sems += [pltpu.SemaphoreType.DMA((2,))] * 5
    out = jax.ShapeDtypeStruct((2, ROWS, D), BF)
    both = pl.pallas_call(
        kernel,
        out_shape=out,
        in_specs=[far] * 10,
        out_specs=far,
        scratch_shapes=[
            pltpu.VMEM((ROWS, D), BF),
            pltpu.VMEM((ROWS, D), BF),
            pltpu.VMEM((ROWS, D), BF),
            pltpu.VMEM((TOP, ROWS), jnp.int32),
            pltpu.VMEM((TOP, ROWS), F32),
            pltpu.VMEM((TOP, ROWS), jnp.int32),
            pltpu.VMEM((TOP, ROWS), F32),
            pltpu.VMEM((1, D), F32),
            pltpu.SemaphoreType.DMA((8,)),
            pltpu.VMEM((2, SIDE - 1, DEEP, ROWS, CH), BF),
            pltpu.VMEM((NOUT, 2, SIDE, DEEP, ROWS, CH), BF),
            pltpu.VMEM((NOUT, 2, SIDE, SIDE, PAIR, CH), BF),
            pltpu.VMEM((RING_S, 2, SIDE - 1, SIDE, PAIR, CH), BF),
            pltpu.VMEM((2, 2, CH, HID), BF),
            pltpu.VMEM((2, 2, HID, CH), BF),
            pltpu.VMEM((RING_O, 2, SIDE, SIDE, PAIR, CH), BF),
            pltpu.VMEM((RING_Z, 2, DEEP, SIDE, ROWS, CH), BF),
            pltpu.VMEM((NRET, 2, SIDE, ROWS, CH), BF),
            pltpu.VMEM((RING_X, 2, SIDE, ROWS, CH), BF),
            pltpu.VMEM((NRET, 2, 2, ROWS, CH), BF),
            pltpu.VMEM((NCH, 2, ROWS, CH), F32),
            pltpu.VMEM((SIDE, LINE, HID), F32),
            pltpu.VMEM((SIDE, LINE, HID), F32),
            pltpu.VMEM((SIDE, LINE, HID), BF),
            pltpu.VMEM((2, 2, SIDE, LINE, PT), BF),
            pltpu.VMEM((2, SIDE, LINE, 128), F32),
            pltpu.VMEM((2, 2, SIDE, 2 * PT, LINE), BF),
            pltpu.VMEM((2, SIDE, 16, PT), F32),
            pltpu.VMEM((2, DEEP, SIDE, 16, PT), F32),
            pltpu.VMEM((2, SIDE, 16, PT), F32),
            pltpu.VMEM((2, SIDE, 16, PT), F32),
            pltpu.VMEM((NRET, 2, 2, DEEP, ROWS // 2, CH), BF),
        ]
        + sems,
        compiler_params=pltpu.CompilerParams(
            collective_id=0, has_side_effects=True, vmem_limit_bytes=63 * 2**20
        ),
        cost_estimate=pl.CostEstimate(flops=30 * 10**9, bytes_accessed=40 * 10**6, transcendentals=2 * 10**6),
    )(
        act_fwd[0], routes_fwd[0].T, mix_fwd[0].T, cot_bwd[0], saved_bwd[0], routes_bwd[0].T, mix_bwd[0].T,
        norm_gain, w_up[0, 0], w_down[0, 0],
    )
    return both[0:1], both[1:2]


def solution(mesh):
    rows = P("pipe", "expert", None)
    return jax.shard_map(
        per_device,
        mesh=mesh,
        in_specs=(rows,) * 7 + (P("pipe", None),) + (P("pipe", "expert", None, None),) * 2,
        out_specs=(rows, rows),
        check_vma=False,
    )
```
